32 devices in a mesh: ctx: 8 (over z, x), head: 4 (over y, core).
Axes of the slice: x: 2, y: 2, z: 4, core: 2. Of those that a mesh axis runs over, the one named last changes fastest.
Arguments:
- queries: bfloat16 [1536, 1024], P(('ctx', 'head')), may hold values from -1.5 to 1.5, as said below
- key_inputs: bfloat16 [1536, 1024], P(('ctx', 'head')), may hold values from -1.5 to 1.5, as said below
- value_inputs: bfloat16 [1536, 1024], P(('ctx', 'head')), may hold values from -6 to 6
- out_grad: bfloat16 [1536, 1024], P(('ctx', 'head')), may hold values from -6 to 6
- attn_output: bfloat16 [1536, 1024], P(('ctx', 'head')), may hold values from -6 to 6
- gate_logits: bfloat16 [1536, 8], P(('ctx', 'head')), may hold values from 0 to 16
- lse: float32 [1536, 8], P(('ctx', 'head')), as said below
Outputs:
- query_grad: bfloat16 [1536, 1024], P(('ctx', 'head'))
- key_grad: bfloat16 [1536, 1024], P(('ctx', 'head'))
- value_grad: bfloat16 [1536, 1024], P(('ctx', 'head'))
- gate_grad: bfloat16 [1536, 8], P(('ctx', 'head'))
The draws below stay inside these ranges and needn't reach their ends.
Inputs may be any that keep to these rules, and one draw needn't show every extreme that they name: `queries`: queries of every token. `key_inputs`: keys of every token. `lse`: the forward pass's log-sum-exp of each query's scores.
All inputs are finite; a program needn't handle non-finite values.
Results may differ from the reference program's by a relative error of at most 0.0052.
Values may be sent and summed in bfloat16 or wider, within the bound.
No kernel may reach another device: no remote copies, remote signals or barrier semaphores. Data moves between devices by JAX's collectives and lax.ppermute only.
A program may use at most 128 MiB of HBM per device.

```python
import math
import jax
import jax.numpy as jnp
from jax import lax

HEAD_GROUP = 8
DH = 128
SEQUENCE_TOKENS = 1536


def key_table(key):
    shared_key = jax.random.fold_in(key, 21)
    return jax.random.uniform(shared_key, (SEQUENCE_TOKENS, HEAD_GROUP * DH), minval=-1.5, maxval=1.5)


def draw_key_inputs(key, part):
    return key_table(key).astype(jnp.float32).astype(jnp.bfloat16)


def query_table(key):
    key = jax.random.fold_in(key, 5)
    own = jax.random.uniform(key, (SEQUENCE_TOKENS, HEAD_GROUP * DH), minval=-1.5, maxval=1.5)
    mixed = own
    return jnp.clip(mixed, -1.5, 1.5).astype(jnp.float32).astype(jnp.bfloat16)


def draw_queries(key, part):
    return query_table(key)


def gate_table(key, fast_share):
    key = jax.random.fold_in(key, 11)
    rapid_random_key, baseline_random_key, jitter_random_key, spike_random_key, retain_random_key, gradual_random_key = jax.random.split(key, 6)
    bell_noise = jnp.clip(0.5 * jax.random.normal(jitter_random_key, (SEQUENCE_TOKENS, HEAD_GROUP)), -1.0, 1.0)
    random_jitter = bell_noise
    fast = jax.random.bernoulli(rapid_random_key, fast_share, (HEAD_GROUP,))
    fast_level = jax.random.uniform(baseline_random_key, (HEAD_GROUP,), minval=jnp.log(30.0), maxval=jnp.log(50.0))
    slow_level = jnp.log(SEQUENCE_TOKENS / (0.3 * jnp.log(10.0))) + jax.random.uniform(gradual_random_key, (HEAD_GROUP,), minval=0.0, maxval=1.6)
    baseline_offset = jnp.where(fast, fast_level, slow_level)
    spike_noise = jax.random.bernoulli(spike_random_key, 2.0 / SEQUENCE_TOKENS, (SEQUENCE_TOKENS, HEAD_GROUP))
    spike_amplitude = jax.random.uniform(retain_random_key, (SEQUENCE_TOKENS, HEAD_GROUP), minval=0.0, maxval=1.4)
    gate_scores_raw = jnp.where(spike_noise, spike_amplitude, baseline_offset[None, :] + random_jitter)
    return gate_scores_raw.astype(jnp.float32).astype(jnp.bfloat16)


def draw_gate_logits(key, part):
    return gate_table(key, 0.5)


def draw_lse(key, part):
    gate_scores_raw = gate_table(key, 0.5)
    key = jax.random.fold_in(key, 13)
    keep = jnp.exp(jax.nn.log_sigmoid(gate_scores_raw.astype(jnp.float32)))

    def step(total, keep_row):
        total = keep_row * total + 1.0
        return (total, total)
    final, totals = lax.scan(step, jnp.zeros((HEAD_GROUP,), jnp.float32), keep)
    jitter = jax.random.uniform(key, (SEQUENCE_TOKENS, HEAD_GROUP), minval=-0.2, maxval=0.2)
    return (jnp.log(totals) + 0.28 + jitter).astype(jnp.float32)


def block_scale(key, dims, cuts, low, top_value):
    loudness, own = 1.0, jax.random.fold_in(key, 6)
    for axis_at, blocks in cuts:
        draws = jnp.exp(jax.random.uniform(jax.random.fold_in(own, axis_at), (blocks,), jnp.float32, low / len(cuts), top_value / len(cuts)))
        loudness = loudness * jnp.repeat(draws, dims[axis_at] // blocks).reshape([-1 if axis == axis_at else 1 for axis in range(len(dims))])
    return loudness


def bell_draw(own_key, extent, scale, most, cuts=(), kind=jnp.bfloat16):
    loudness = block_scale(own_key, extent, cuts, -0.22, 0.18) if cuts else 1.0
    drawn = jax.random.normal(own_key, extent, jnp.float32) * scale * loudness
    return jnp.minimum(jnp.maximum(drawn, -most), most).astype(kind)


def setup_inputs(seed: int = 0) -> dict:
    key_of = jax.random.split(jax.random.key(seed), 8)
    queries = draw_queries(jax.random.fold_in(key_of[7], 71), 0)
    key_inputs = draw_key_inputs(jax.random.fold_in(key_of[7], 71), 0)
    value_inputs = bell_draw(key_of[2], (SEQUENCE_TOKENS, HEAD_GROUP * DH), 1.0, 6.0, ((0, 32),))
    out_grad = bell_draw(key_of[3], (SEQUENCE_TOKENS, HEAD_GROUP * DH), 1.0, 6.0, ((0, 32),))
    attn_output = bell_draw(key_of[4], (SEQUENCE_TOKENS, HEAD_GROUP * DH), 1.0, 6.0, ((0, 32),))
    gate_logits = draw_gate_logits(jax.random.fold_in(key_of[7], 71), 0)
    lse = draw_lse(jax.random.fold_in(key_of[7], 71), 0)
    return dict(queries=queries, key_inputs=key_inputs, value_inputs=value_inputs, out_grad=out_grad, attn_output=attn_output, gate_logits=gate_logits, lse=lse)


def head_backward(items):
    query_head, key_head, value_head, grad_head, output_head, curve_head, lse_head = items
    score_scale = DH ** -0.5
    block_len = math.gcd(SEQUENCE_TOKENS, 1024)
    block_count = SEQUENCE_TOKENS // block_len
    key_pos = jnp.arange(SEQUENCE_TOKENS, dtype=jnp.int32)

    def one_block(carry_in, block_index):
        key_acc, value_acc, column_acc = carry_in
        first_row = block_index * block_len
        query_blk = lax.dynamic_slice_in_dim(query_head, first_row, block_len, 0)
        grad_blk = lax.dynamic_slice_in_dim(grad_head, first_row, block_len, 0)
        output_blk = lax.dynamic_slice_in_dim(output_head, first_row, block_len, 0)
        curve_blk = lax.dynamic_slice_in_dim(curve_head, first_row, block_len, 0)
        lse_blk = lax.dynamic_slice_in_dim(lse_head, first_row, block_len, 0)
        query_pos = first_row + jnp.arange(block_len, dtype=jnp.int32)
        causal = key_pos[None, :] <= query_pos[:, None]
        scores = score_scale * jnp.dot(query_blk, key_head.T, preferred_element_type=jnp.float32) + curve_blk[:, None] - curve_head[None, :]
        probs = jnp.where(causal, jnp.exp(scores - lse_blk[:, None]), 0.0)
        row_delta = jnp.sum(grad_blk.astype(jnp.float32) * output_blk.astype(jnp.float32), axis=1)
        grad_probs = jnp.dot(grad_blk, value_head.T, preferred_element_type=jnp.float32)
        score_grad = probs * (grad_probs - row_delta[:, None])
        score_half = score_grad.astype(jnp.bfloat16)
        probs_half = probs.astype(jnp.bfloat16)
        query_part = score_scale * jnp.dot(score_half, key_head, preferred_element_type=jnp.float32)
        key_acc = key_acc + jnp.dot(score_half.T, query_blk, preferred_element_type=jnp.float32)
        value_acc = value_acc + jnp.dot(probs_half.T, grad_blk, preferred_element_type=jnp.float32)
        column_acc = column_acc + jnp.sum(score_grad, axis=0)
        return (key_acc, value_acc, column_acc), (query_part, jnp.sum(score_grad, axis=1))

    zero_rows = jnp.zeros((SEQUENCE_TOKENS, DH), jnp.float32)
    start = (zero_rows, zero_rows, jnp.zeros((SEQUENCE_TOKENS,), jnp.float32))
    (key_acc, value_acc, column_acc), (query_parts, row_parts) = lax.scan(one_block, start, jnp.arange(block_count, dtype=jnp.int32))
    query_grad = query_parts.reshape(SEQUENCE_TOKENS, DH)
    curve_grad = row_parts.reshape(SEQUENCE_TOKENS) - column_acc
    return query_grad, score_scale * key_acc, value_acc, curve_grad


def reference(queries, key_inputs, value_inputs, out_grad, attn_output, gate_logits, lse):
    def by_head(array):
        return array.reshape(SEQUENCE_TOKENS, HEAD_GROUP, DH).transpose(1, 0, 2)

    gate_float = gate_logits.astype(jnp.float32)
    log_gates = jax.nn.log_sigmoid(gate_float)
    curve = jnp.cumsum(log_gates, axis=0)
    query_grad, key_grad, value_grad, curve_grad = lax.map(head_backward, (by_head(queries), by_head(key_inputs), by_head(value_inputs), by_head(out_grad), by_head(attn_output), curve.T, lse.T))
    gate_sum = jnp.flip(jnp.cumsum(jnp.flip(curve_grad, 1), axis=1), 1)
    gate_grad = (gate_sum.T * jax.nn.sigmoid(-gate_float)).astype(jnp.bfloat16)

    def merged(array):
        return array.transpose(1, 0, 2).reshape(SEQUENCE_TOKENS, HEAD_GROUP * DH).astype(jnp.bfloat16)

    return merged(query_grad), merged(key_grad), merged(value_grad), gate_grad
```

```python
import functools
import math

import jax
import jax.numpy as jnp
from jax import lax
from jax.experimental import pallas as pl
from jax.experimental.pallas import tpu as pltpu
from jax.sharding import PartitionSpec as P

BF16 = jnp.bfloat16
F32 = jnp.float32
LANES = 128
STAT = 16
EXACT = lax.Precision.HIGHEST
VMEM = pl.BlockSpec(memory_space=pltpu.VMEM)
SMEM = pl.BlockSpec(memory_space=pltpu.SMEM)
HBM = pl.BlockSpec(memory_space=pltpu.HBM)


def iota(shape, dim):
    return lax.broadcasted_iota(jnp.int32, shape, dim)


def dot_exact(a, b):
    return jnp.dot(a, b, precision=EXACT, preferred_element_type=F32)


def split3(x):
    hi = x.astype(BF16).astype(F32)
    rest = x - hi
    mid = rest.astype(BF16).astype(F32)
    low = (rest - mid).astype(BF16).astype(F32)
    return hi, mid, low


def stack_rows(rows):
    at = iota((STAT, LANES), 0)
    block = jnp.zeros((STAT, LANES), F32)
    for j, row in enumerate(rows):
        block = jnp.where(at == j, jnp.broadcast_to(row, (STAT, LANES)), block)
    return block


def pad_rows(x):
    missing = LANES - x.shape[0]
    if missing:
        x = jnp.concatenate([x, jnp.zeros((missing, x.shape[1]), x.dtype)], axis=0)
    return x


def wrap(x, n):
    x = jnp.where(x < 0, x + n, x)
    return jnp.where(x >= n, x - n, x)


def block_positions(ids, shape, dim, heads, stride, first, sources):
    index = iota(shape, dim)
    pos = jnp.full(shape, -1, jnp.int32)
    for at, src in enumerate(sources):
        begin = first + at * heads
        here = (index >= begin) & (index < begin + heads)
        place = wrap(ids[0] - (index - begin), heads)
        pos = jnp.where(here, ids[1 + src] + place * stride, pos)
    return pos


def pack_kernel(ids, *refs):
    sources, refs = (refs[:7], refs[7:])
    heads, rows = sources[5].shape
    query_out, key_out = (refs[:heads], refs[heads : 2 * heads])
    *held, gate_wide, lse_wide, sems = refs[2 * heads :]
    copies = [pltpu.make_async_copy(src, dst, sems.at[i]) for i, (src, dst) in enumerate(zip(sources, held))]
    for i in (5, 6, 3, 4, 0, 1, 2):
        copies[i].start()
    q_ref, k_ref, v_ref, g_ref, o_ref, gate_ref, lse_ref = held
    copies[5].wait()
    copies[6].wait()
    gate_wide[...] = jnp.zeros_like(gate_wide)
    lse_wide[...] = jnp.zeros_like(lse_wide)
    gate_wide[:, 0:rows] = gate_ref[...].astype(F32)
    lse_wide[:, 0:rows] = lse_ref[...]
    copies[3].wait()
    copies[4].wait()

    columns = [pl.ds(pl.multiple_of(wrap(ids[0] + k, heads) * LANES, LANES), LANES) for k in range(heads)]
    lane = iota((rows, LANES), 1)
    delta = jnp.zeros((rows, LANES), F32)
    for k in range(heads):
        grad = g_ref[:, columns[k]]
        row_sum = jnp.sum(grad.astype(F32) * o_ref[:, columns[k]].astype(F32), axis=1, keepdims=True)
        delta = jnp.where(lane == k, row_sum, delta)
        query_out[k][rows : 2 * rows, :] = grad
    delta = split3(pad_rows(delta).T)
    for k in range(heads):
        at = pl.ds(wrap(ids[0] + k, heads), 1)
        parts = [gate_wide[at, :], *split3(lse_wide[at, :]), *[part[k : k + 1] for part in delta]]
        query_out[k][2 * rows :, :] = stack_rows(parts).astype(BF16)
    copies[0].wait()
    for k in range(heads):
        query_out[k][0:rows, :] = q_ref[:, columns[k]]
    copies[1].wait()
    copies[2].wait()
    for k in range(heads):
        key_out[k][0:rows, :] = k_ref[:, columns[k]]
        key_out[k][rows:, :] = v_ref[:, columns[k]]


def join_kernel(*refs):
    outs = [ref for ref in refs if len(ref.shape) == 3]
    chunks = [ref for ref in refs if len(ref.shape) == 2]
    for k, chunk in enumerate(chunks):
        begin = 0
        for out in outs:
            out[k] = chunk[begin : begin + out.shape[1], :]
            begin += out.shape[1]


def stat_kernel(plan, ids, *refs):
    rows, heads, across, down, stride, scale = plan
    count = across * down
    stat_refs = refs[:count]
    score_ref, delta_ref, keep_ref = refs[count:]

    def row_of(src, j):
        block = stat_refs[src][...].astype(F32)
        return jnp.concatenate([block[k, j : j + 1, :] for k in range(heads)], axis=0)

    gates = [row_of(src, 0) for src in range(count)]
    valid = iota((heads, LANES), 1) < rows
    logs = [
        jnp.where(valid, jnp.minimum(x, 0.0) - jnp.log1p(jnp.exp(-jnp.abs(x))), 0.0) for x in gates
    ]
    logs = jnp.concatenate(logs, axis=0)
    blocks = count * heads
    square = (LANES, LANES)
    upto = (iota(square, 0) <= iota(square, 1)).astype(F32)
    order = range(count)
    earlier = block_positions(ids, (blocks, blocks), 1, heads, stride, 0, order) < block_positions(
        ids, (blocks, blocks), 0, heads, stride, 0, order
    )
    before = jnp.sum(dot_exact(earlier.astype(F32), logs), axis=1, keepdims=True)
    curve = dot_exact(logs, upto) + before

    def curve_of(src):
        return curve[src * heads : (src + 1) * heads]

    zero = jnp.zeros((heads, LANES), F32)
    for m in range(score_ref.shape[0]):
        q_rows, d_rows, k_rows = [], [], []
        for s in (2 * m, 2 * m + 1):
            if s < down:
                src = s * across
                lse = row_of(src, 1) + row_of(src, 2) + row_of(src, 3)
                q_rows += [*split3((curve_of(src) - lse) / scale), zero]
                d_rows += [-row_of(src, 4), -row_of(src, 5), -row_of(src, 6), zero]
            else:
                q_rows += [zero] * 4
                d_rows += [zero] * 4
            k_rows += [*split3(-curve_of(s) / scale), zero] if s < across else [zero] * 4
        score_ref[m] = jnp.concatenate(q_rows + k_rows, axis=0).T[:rows]
        delta_ref[m] = pad_rows(jnp.concatenate(d_rows, axis=0)).T[:rows]
    keep_ref[...] = 1.0 / (1.0 + jnp.exp(gates[0]))


def attention_kernel(plan, ids, *refs):
    rows, heads, across, down, stride, scale, static_order = plan
    q_src, refs = (refs[:down], refs[down:])
    k_src, refs = (refs[:across], refs[across:])
    score_ref, delta_ref, refs = (refs[0], refs[1], refs[2:])
    dq_own, dk_own, dv_own, sums_ref, refs = (*refs[:4], refs[4:])
    to_down, refs = (refs[: down - 1], refs[down - 1 :])
    to_across, refs = (refs[: across - 1], refs[across - 1 :])
    qe, ge, ke, ve, dq_acc, dk_acc, dv_acc = refs

    lane = iota((rows, LANES), 1)
    half = 8 * heads
    upper = (lane >= half).astype(F32)
    lower = (lane < half).astype(F32)
    ones = jnp.ones((rows, LANES), BF16)

    def slot(s, k, start):
        inner = lane - start - (s % 2) * 4 * heads
        return (inner >= 0) & (inner < 4 * heads) & (lane % heads == k)

    def rows_at(k, s, sources):
        begin = (wrap(ids[0] - k, heads) * sources + s) * rows
        return pl.ds(pl.multiple_of(begin, math.gcd(rows, 128)), rows)

    for k in range(heads):
        for s in range(down):
            at = rows_at(k, s, down)
            mine = slot(s, k, 0)
            qe[at, 0:LANES] = q_src[s][k, 0:rows, :]
            qe[at, LANES:] = jnp.where(mine, score_ref[s // 2], upper).astype(BF16)
            ge[at, 0:LANES] = q_src[s][k, rows : 2 * rows, :]
            ge[at, LANES:] = jnp.where(mine, delta_ref[s // 2], 0.0).astype(BF16)
        for s in range(across):
            at = rows_at(k, s, across)
            mine = slot(s, k, half)
            ke[at, 0:LANES] = k_src[s][k, 0:rows, :]
            ke[at, LANES:] = jnp.where(mine, score_ref[s // 2], lower).astype(BF16)
            ve[at, 0:LANES] = k_src[s][k, rows : 2 * rows, :]
            ve[at, LANES:] = ones

    pair = 2
    wide, tall = (pair * down * rows, pair * across * rows)
    step = pair * stride * rows

    def token_pos(shape, dim, sources):
        index = iota(shape, dim)
        pos = jnp.zeros(shape, jnp.int32)
        for c in range(pair):
            for s, src in enumerate(sources):
                first = (c * len(sources) + s) * rows
                here = (index >= first) & (index < first + rows)
                pos = jnp.where(here, (ids[1 + src] + c * stride) * rows + index - first, pos)
        return pos

    ahead = token_pos((1, wide), 1, range(0, down * across, across)) - token_pos(
        (tall, 1), 0, range(across)
    )
    factor = scale * math.log2(math.e)
    nt = (((1,), (1,)), ((), ()))
    tn = (((0,), (0,)), ((), ()))

    def tile(col_at, row_at, allowed):
        q_part, g_part = (qe[row_at, :], ge[row_at, :])
        k_part, v_part = (ke[col_at, :], ve[col_at, :])
        scores = lax.dot_general(k_part, q_part, nt, preferred_element_type=F32)
        shifted = lax.dot_general(v_part, g_part, nt, preferred_element_type=F32)
        probs = jnp.exp2(scores * factor)
        if allowed is not None:
            probs = jnp.where(allowed, probs, 0.0)
        grads = (probs * shifted).astype(BF16)
        probs = probs.astype(BF16)
        dv = jnp.dot(probs, g_part[:, 0:LANES], preferred_element_type=F32)
        dk = jnp.dot(grads, q_part, preferred_element_type=F32)
        dq = lax.dot_general(grads, k_part, tn, preferred_element_type=F32)
        return dq, dk, dv

    groups = heads // pair
    if static_order:
        for kc in range(groups):
            col_at = pl.ds(kc * tall, tall)
            diag_at = pl.ds(kc * wide, wide)
            dq, dk, dv = tile(col_at, diag_at, ahead >= 0)
            dq_acc[diag_at, :] = dq if kc == 0 else dq_acc[diag_at, :] + dq
            if kc + 1 < groups:
                rest_at = pl.ds((kc + 1) * wide, (groups - 1 - kc) * wide)
                dq, dk2, dv2 = tile(col_at, rest_at, None)
                dq_acc[rest_at, :] = dq if kc == 0 else dq_acc[rest_at, :] + dq
                dk, dv = (dk + dk2, dv + dv2)
            dk_acc[col_at, :] = dk
            dv_acc[col_at, :] = dv
    else:
        dq_acc[...] = jnp.zeros_like(dq_acc)
        dk_acc[...] = jnp.zeros_like(dk_acc)
        dv_acc[...] = jnp.zeros_like(dv_acc)

        @pl.loop(0, groups)
        def _(kc):
            @pl.loop(0, groups)
            def _(kr):
                col_at = pl.ds(pl.multiple_of(kc * tall, tall), tall)
                row_at = pl.ds(pl.multiple_of(kr * wide, wide), wide)
                dq, dk, dv = tile(col_at, row_at, ahead >= (kc - kr) * step)
                dq_acc[row_at, :] += dq
                dk_acc[col_at, :] += dk
                dv_acc[col_at, :] += dv

    sums = jnp.zeros((rows, LANES), F32)
    for k in range(heads):
        for s in range(down):
            at = rows_at(k, s, down)
            dq = dq_acc[at, 0:LANES]
            sums = jnp.where(lane == s * heads + k, dq_acc[at, LANES:], sums)
            if s == 0:
                dq_own[k] = dq
            else:
                to_down[s - 1][k] = dq.astype(BF16)
        for s in range(across):
            at = rows_at(k, s, across)
            dk, dv = (dk_acc[at, 0:LANES], dv_acc[at, :])
            sums = jnp.where(lane == half + s * heads + k, -dk_acc[at, LANES:], sums)
            if s == 0:
                dk_own[k] = dk
                dv_own[k] = dv
            else:
                to_across[s - 1][k, 0:rows, :] = dk.astype(BF16)
                to_across[s - 1][k, rows:, :] = dv.astype(BF16)
    sums_ref[...] = sums


def suffix_kernel(plan, ids, sums_ref, own_ref, *others):
    rows, heads, across, down, stride = plan
    count = across * down
    blocks = count * heads
    square = (LANES, LANES)
    turned = pad_rows(sums_ref[...]).T
    onward = (iota(square, 0) >= iota(square, 1)).astype(F32)
    shape = (blocks, LANES)
    slot_pos = jnp.maximum(
        block_positions(ids, shape, 1, heads, stride, 0, range(0, count, across)),
        block_positions(ids, shape, 1, heads, stride, 8 * heads, range(across)),
    )
    target_pos = block_positions(ids, shape, 0, heads, stride, 0, range(count))
    later = dot_exact((slot_pos > target_pos).astype(F32), turned)
    inner = dot_exact((slot_pos == target_pos).astype(F32), turned)
    suffix = jnp.sum(later, axis=1, keepdims=True) + dot_exact(inner, onward)
    own_ref[...] = suffix[0:heads]
    for src in range(1, count):
        parts = split3(suffix[src * heads : (src + 1) * heads])
        for k in range(heads):
            others[src - 1][k] = stack_rows([part[k : k + 1] for part in parts]).astype(BF16)


def combine_keys_kernel(scale, dk_ref, dv_ref, *refs):
    heads, rows, _ = dk_ref.shape
    outs, received = (refs[-heads:], refs[:-heads])
    for k in range(heads):
        dk, dv = (dk_ref[k], dv_ref[k])
        for ref in received:
            dk += ref[k, 0:rows, :].astype(F32)
            dv += ref[k, rows:, :].astype(F32)
        outs[k][0:rows, :] = (scale * dk).astype(BF16)
        outs[k][rows:, :] = dv.astype(BF16)


def combine_queries_kernel(scale, down, dq_ref, gate_ref, keep_ref, *refs):
    heads, rows, _ = dq_ref.shape
    outs, received = (refs[-heads:], refs[:-heads])
    for k in range(heads):
        dq = dq_ref[k]
        for ref in received[: down - 1]:
            dq += ref[k].astype(F32)
        total = gate_ref[k : k + 1, :]
        extra = jnp.zeros((STAT, LANES), F32)
        for ref in received[down - 1 :]:
            extra += ref[k].astype(F32)
        gate = (total + jnp.sum(extra, axis=0, keepdims=True)) * keep_ref[k : k + 1, :]
        outs[k][0:rows, :] = (scale * dq).astype(BF16)
        outs[k][rows:, :] = jnp.broadcast_to(gate, (STAT, LANES)).astype(BF16)


def unpack_kernel(ids, *refs):
    heads = (len(refs) - 4) // 2
    queries, keys = (refs[:heads], refs[heads : 2 * heads])
    dq_ref, dk_ref, dv_ref, gate_ref = refs[2 * heads :]
    rows = dq_ref.shape[0]
    at = iota((heads, LANES), 0)
    gates = jnp.zeros((heads, LANES), F32)
    for k in range(heads):
        head = wrap(ids[0] + k, heads)
        cols = pl.ds(pl.multiple_of(head * LANES, LANES), LANES)
        dq_ref[:, cols] = queries[k][0:rows, :]
        dk_ref[:, cols] = keys[k][0:rows, :]
        dv_ref[:, cols] = keys[k][rows:, :]
        row = queries[k][rows:, :].astype(F32)[0:1]
        gates = jnp.where(at == head, jnp.broadcast_to(row, (heads, LANES)), gates)
    gate_ref[...] = gates[:, 0:rows].astype(BF16)


def struct(shape, dtype=BF16):
    return jax.ShapeDtypeStruct(shape, dtype)


def call(kernel, out_shape, inputs, scratch=(), smem=0, space=VMEM):
    return pl.pallas_call(
        kernel,
        out_shape=out_shape,
        in_specs=[SMEM] * smem + [space] * (len(inputs) - smem),
        out_specs=jax.tree.map(lambda _: VMEM, out_shape),
        scratch_shapes=list(scratch),
        compiler_params=pltpu.CompilerParams(vmem_limit_bytes=40 * 1024 * 1024),
    )(*inputs)


def per_device(queries, key_inputs, value_inputs, out_grad, attn_output, gate_logits, lse):
    ctx, group = (lax.axis_size("ctx"), lax.axis_size("head"))
    rows, heads = gate_logits.shape
    width = queries.shape[1]
    scale = (width // heads) ** -0.5
    sub = ctx // heads
    count = sub * group
    across = max(d for d in range(1, count + 1) if count % d == 0 and d * d <= count)
    down = count // across
    both = ("ctx", "head")

    def device_of(head, p):
        return ((p // group) * heads + head) * group + p % group

    def shift(array, sb, sa):
        pairs = []
        for head in range(heads):
            for b in range(down):
                for a in range(across):
                    source = ((b + sb) % down) * across + (a + sa) % across
                    pairs.append((device_of(head, source), device_of(head, b * across + a)))
        return lax.ppermute(array, both, pairs)

    def turn(chunks, sign):
        moved = [chunks[0]]
        for k in range(1, heads):
            pairs = [
                (device_of(head, p), device_of((head + sign * k) % heads, p))
                for head in range(heads)
                for p in range(count)
            ]
            moved.append(lax.ppermute(chunks[k], both, pairs))
        return moved

    here = lax.axis_index("ctx")
    member = (here // heads) * group + lax.axis_index("head")
    my_b, my_a = (member // across, member % across)
    ids = [here % heads]
    for sb in range(down):
        for sa in range(across):
            p = ((my_b + sb) % down) * across + (my_a + sa) % across
            ids.append((p // group) * heads * group + p % group)
    ids = jnp.stack(ids).astype(jnp.int32)
    members = [(sb, sa) for sb in range(down) for sa in range(across)]

    chunks = call(
        pack_kernel,
        [struct((2 * rows + STAT, LANES))] * heads + [struct((2 * rows, LANES))] * heads,
        (ids, queries, key_inputs, value_inputs, out_grad, attn_output, gate_logits.T, lse.T),
        scratch=[pltpu.VMEM((rows, width), BF16)] * 5
        + [pltpu.VMEM((heads, rows), BF16), pltpu.VMEM((heads, rows), F32)]
        + [pltpu.VMEM((heads, LANES), F32)] * 2
        + [pltpu.SemaphoreType.DMA((7,))],
        smem=1,
        space=HBM,
    )
    query_chunks = turn(chunks[:heads], 1)
    key_chunks = turn(chunks[heads:], 1)
    pieces = struct((heads, 2 * rows, LANES))
    query_own, stat_own = call(join_kernel, [pieces, struct((heads, STAT, LANES))], query_chunks)
    stat_all = [stat_own if m == (0, 0) else shift(stat_own, *m) for m in members]
    query_all = [query_own] + [shift(query_own, sb, 0) for sb in range(1, down)]
    (key_own,) = call(join_kernel, [pieces], key_chunks)
    key_all = [key_own] + [shift(key_own, 0, sa) for sa in range(1, across)]

    chunk_count = -(-max(across, down) // 2)
    extras = struct((chunk_count, rows, LANES), F32)
    score_cols, delta_cols, keep = call(
        functools.partial(stat_kernel, (rows, heads, across, down, group, scale)),
        [extras, extras, struct((heads, LANES), F32)],
        (ids, *stat_all),
        smem=1,
    )
    wide, tall = (heads * down * rows, heads * across * rows)
    piece = (heads, rows, LANES)
    dq_own, dk_own, dv_own, sums, *partial = call(
        functools.partial(attention_kernel, (rows, heads, across, down, group, scale, sub == 1)),
        [struct(piece, F32)] * 3
        + [struct((rows, LANES), F32)]
        + [struct(piece)] * (down - 1)
        + [pieces] * (across - 1),
        (ids, *query_all, *key_all, score_cols, delta_cols),
        scratch=[
            pltpu.VMEM((wide, 2 * LANES), BF16),
            pltpu.VMEM((wide, 2 * LANES), BF16),
            pltpu.VMEM((tall, 2 * LANES), BF16),
            pltpu.VMEM((tall, 2 * LANES), BF16),
            pltpu.VMEM((wide, 2 * LANES), F32),
            pltpu.VMEM((tall, 2 * LANES), F32),
            pltpu.VMEM((tall, LANES), F32),
        ],
        smem=1,
    )
    key_back = [shift(partial[down - 2 + sa], 0, across - sa) for sa in range(1, across)]
    query_back = [shift(partial[sb - 1], down - sb, 0) for sb in range(1, down)]
    gate_own, *gate_parts = call(
        functools.partial(suffix_kernel, (rows, heads, across, down, group)),
        [struct((heads, LANES), F32)] + [struct((heads, STAT, LANES))] * (count - 1),
        (ids, sums),
        smem=1,
    )
    gate_back = [
        shift(part, (down - sb) % down, (across - sa) % across)
        for part, (sb, sa) in zip(gate_parts, members[1:])
    ]
    key_grads = call(
        functools.partial(combine_keys_kernel, scale),
        [struct((2 * rows, LANES))] * heads,
        (dk_own, dv_own, *key_back),
    )
    key_grads = turn(key_grads, -1)
    query_grads = call(
        functools.partial(combine_queries_kernel, scale, down),
        [struct((rows + STAT, LANES))] * heads,
        (dq_own, gate_own, keep, *query_back, *gate_back),
    )
    query_grads = turn(query_grads, -1)
    full = struct(queries.shape)
    dq, dk, dv, gate_grad = call(
        unpack_kernel,
        [full, full, full, struct((heads, rows))],
        (ids, *query_grads, *key_grads),
        smem=1,
    )
    return dq, dk, dv, gate_grad.T


def solution(mesh):
    split = P(("ctx", "head"), None)
    return jax.shard_map(
        per_device,
        mesh=mesh,
        in_specs=(split,) * 7,
        out_specs=(split,) * 4,
        check_vma=False,
    )
```

```python
import functools
import math

import jax
import jax.numpy as jnp
from jax import lax
from jax.experimental import pallas as pl
from jax.experimental.pallas import tpu as pltpu
from jax.sharding import PartitionSpec as P

BF16 = jnp.bfloat16
F32 = jnp.float32
LANES = 128
STAT = 16
EXACT = lax.Precision.HIGHEST
VMEM = pl.BlockSpec(memory_space=pltpu.VMEM)
SMEM = pl.BlockSpec(memory_space=pltpu.SMEM)
HBM = pl.BlockSpec(memory_space=pltpu.HBM)
PACK_LIMIT = 64


def iota(shape, dim):
    return lax.broadcasted_iota(jnp.int32, shape, dim)


def dot_exact(a, b):
    return jnp.dot(a, b, precision=EXACT, preferred_element_type=F32)


def split3(x):
    hi = x.astype(BF16).astype(F32)
    rest = x - hi
    mid = rest.astype(BF16).astype(F32)
    low = (rest - mid).astype(BF16).astype(F32)
    return hi, mid, low


def stack_rows(rows):
    at = iota((STAT, LANES), 0)
    block = jnp.zeros((STAT, LANES), F32)
    for j, row in enumerate(rows):
        block = jnp.where(at == j, jnp.broadcast_to(row, (STAT, LANES)), block)
    return block


def pad_rows(x):
    missing = LANES - x.shape[0]
    if missing:
        x = jnp.concatenate([x, jnp.zeros((missing, x.shape[1]), x.dtype)], axis=0)
    return x


def wrap(x, n):
    return jnp.where(x >= n, x - n, x)


KIND, HALF, MEMBER, BASE = range(4)


def block_positions(ids, shape, dim, heads, stride, first, sources):
    index = iota(shape, dim)
    pos = jnp.full(shape, -1, jnp.int32)
    for at, src in enumerate(sources):
        begin = first + at * heads
        here = (index >= begin) & (index < begin + heads)
        pos = jnp.where(here, ids[BASE + src] + (index - begin) * stride, pos)
    return pos


def pack_kernel(*refs):
    sources, out_ref, refs = (refs[:7], refs[7], refs[8:])
    heads, rows = sources[5].shape
    *held, gate_wide, lse_wide, sems = refs
    copies = [pltpu.make_async_copy(src, dst, sems.at[i]) for i, (src, dst) in enumerate(zip(sources, held))]
    for i in (5, 6, 3, 4, 0, 1, 2):
        copies[i].start()
    q_ref, k_ref, v_ref, g_ref, o_ref, gate_ref, lse_ref = held
    copies[5].wait()
    copies[6].wait()
    gate_wide[...] = jnp.zeros_like(gate_wide)
    lse_wide[...] = jnp.zeros_like(lse_wide)
    gate_wide[:, 0:rows] = gate_ref[...].astype(F32)
    lse_wide[:, 0:rows] = lse_ref[...]
    copies[3].wait()
    copies[4].wait()
    lane = iota((rows, LANES), 1)
    delta = jnp.zeros((rows, LANES), F32)
    for h in range(heads):
        cols = pl.ds(h * LANES, LANES)
        grad = g_ref[:, cols]
        row_sum = jnp.sum(grad.astype(F32) * o_ref[:, cols].astype(F32), axis=1, keepdims=True)
        delta = jnp.where(lane == h, row_sum, delta)
        out_ref[h, rows : 2 * rows, :] = grad
    parts = [gate_wide[...], *split3(lse_wide[...]), *split3(pad_rows(delta).T[:heads])]
    for h in range(heads):
        block = stack_rows([part[h : h + 1] for part in parts])
        out_ref[h, 2 * rows : 2 * rows + STAT, :] = block.astype(BF16)
    for i, ref, first in ((0, q_ref, 0), (1, k_ref, 2 * rows + STAT), (2, v_ref, 3 * rows + STAT)):
        copies[i].wait()
        for h in range(heads):
            out_ref[h, first : first + rows, :] = ref[:, pl.ds(h * LANES, LANES)]


def attention_kernel(plan, ids, own_ref, *refs):
    rows, heads, members, scale = plan
    peers, cross, corner, refs = (
        refs[: members - 1],
        refs[members - 1],
        refs[members : 2 * members - 1],
        refs[2 * members - 1 :],
    )
    outs, scratch = (refs[: 6 + 2 * (members - 1)], refs[6 + 2 * (members - 1) :])
    for kind in (0, 1):

        @pl.when(ids[KIND] == kind)
        def _(kind=kind):
            attention_body(plan, kind, ids, own_ref, peers, cross, corner, outs, scratch)


def attention_body(plan, kind, ids, own_ref, peers, cross, corner, outs, scratch):
    rows, heads, members, scale = plan
    dq_own, dk_own, dv_own, gate_own, keep_own, to_cross = outs[:6]
    to_peer, to_corner = (outs[6 : 5 + members], outs[5 + members :])
    full_1, full_2, some_1, some_2, full_acc, some_acc, value_acc = scratch
    wanted = ids[HALF] == kind
    count = 2 * members
    stat_at = 2 * rows
    peer_stat, cross_stat = ((0, stat_at) if kind == 0 else (stat_at, 0))

    def stat_block(src):
        if src == 0:
            block = own_ref[:, stat_at : stat_at + STAT, :]
        elif src < members:
            block = peers[src - 1][:, peer_stat : peer_stat + STAT, :]
        elif src == members:
            block = cross[:, cross_stat : cross_stat + STAT, :]
        else:
            block = corner[src - members - 1][...]
        return block.astype(F32)

    stats = [stat_block(src) for src in range(count)]

    def row_of(src, j):
        return jnp.concatenate([stats[src][k, j : j + 1, :] for k in range(heads)], axis=0)

    gates = [row_of(src, 0) for src in range(count)]
    in_row = iota((heads, LANES), 1) < rows
    logs = []
    for src, x in enumerate(gates):
        log_gate = jnp.minimum(x, 0.0) - jnp.log1p(jnp.exp(-jnp.abs(x)))
        held = in_row if src < members else in_row & wanted
        logs.append(jnp.where(held, log_gate, 0.0))
    logs = jnp.concatenate(logs, axis=0)
    blocks = count * heads
    square = (LANES, LANES)
    upto = (iota(square, 0) <= iota(square, 1)).astype(F32)
    row_pos = block_positions(ids, (blocks, blocks), 0, heads, members, 0, range(count))
    lane_pos = block_positions(ids, (blocks, blocks), 1, heads, members, 0, range(count))
    before = jnp.sum(dot_exact((lane_pos < row_pos).astype(F32), logs), axis=1, keepdims=True)
    curve = dot_exact(logs, upto) + before

    def curve_of(src):
        return curve[src * heads : (src + 1) * heads]

    all_members, pair = (list(range(members)), [0, members])
    q_sources, k_sources = ((pair, all_members) if kind == 0 else (all_members, pair))
    zero = jnp.zeros((heads, LANES), F32)
    score_cols, delta_cols = [], []
    for m in range(-(-max(members, 2) // 2)):
        q_rows, d_rows, k_rows = [], [], []
        for s in (2 * m, 2 * m + 1):
            if s < len(q_sources):
                src = q_sources[s]
                lse = row_of(src, 1) + row_of(src, 2) + row_of(src, 3)
                q_rows += [*split3((curve_of(src) - lse) / scale), zero]
                d_rows += [-row_of(src, 4), -row_of(src, 5), -row_of(src, 6), zero]
            else:
                q_rows += [zero] * 4
                d_rows += [zero] * 4
            if s < len(k_sources):
                k_rows += [*split3(-curve_of(k_sources[s]) / scale), zero]
            else:
                k_rows += [zero] * 4
        score_cols.append(jnp.concatenate(q_rows + k_rows, axis=0).T[:rows])
        delta_cols.append(pad_rows(jnp.concatenate(d_rows, axis=0)).T[:rows])

    lane = iota((rows, LANES), 1)
    half = 8 * heads
    upper = (lane >= half).astype(F32)
    lower = (lane < half).astype(F32)
    ones = jnp.ones((rows, LANES), BF16)

    def slot(s, k, start):
        inner = lane - start - (s % 2) * 4 * heads
        return (inner >= 0) & (inner < 4 * heads) & (lane % heads == k)

    def full_at(k, s):
        begin = (k * members + wrap(ids[MEMBER] + s, members)) * rows
        return pl.ds(pl.multiple_of(begin, math.gcd(rows, LANES)), rows)

    def some_at(k, s):
        return pl.ds((s * heads + k) * rows, rows)

    def pieces(src, query_side):
        if src == 0:
            return own_ref, 0 if query_side else stat_at + STAT
        return (cross if src == members else peers[src - 1]), 0 if query_side else STAT

    (q_1, q_2, q_at), (k_1, k_2, k_at) = (full_1, full_2, full_at), (some_1, some_2, some_at)
    if kind == 0:
        (q_1, q_2, q_at), (k_1, k_2, k_at) = (k_1, k_2, k_at), (q_1, q_2, q_at)
    for k in range(heads):
        for s, src in enumerate(q_sources):
            array, first = pieces(src, True)
            mine = slot(s, k, 0)
            q_1[q_at(k, s), 0:LANES] = array[k, first : first + rows, :]
            q_1[q_at(k, s), LANES:] = jnp.where(mine, score_cols[s // 2], upper).astype(BF16)
            q_2[q_at(k, s), 0:LANES] = array[k, first + rows : first + 2 * rows, :]
            q_2[q_at(k, s), LANES:] = jnp.where(mine, delta_cols[s // 2], 0.0).astype(BF16)
        for s, src in enumerate(k_sources):
            array, first = pieces(src, False)
            mine = slot(s, k, half)
            k_1[k_at(k, s), 0:LANES] = array[k, first : first + rows, :]
            k_1[k_at(k, s), LANES:] = jnp.where(mine, score_cols[s // 2], lower).astype(BF16)
            k_2[k_at(k, s), 0:LANES] = array[k, first + rows : first + 2 * rows, :]
            k_2[k_at(k, s), LANES:] = ones

    factor = scale * math.log2(math.e)
    nt = (((1,), (1,)), ((), ()))
    tn = (((0,), (0,)), ((), ()))
    own_rows, slot_rows = (heads * rows, members * rows)
    full_rows = heads * slot_rows

    def some_pos(begin, size):
        index = iota((1, size), 1) + begin
        pos = index + ids[MEMBER] * rows
        for k in range(1, heads):
            pos = jnp.where(index >= k * rows, pos + (slot_rows - rows), pos)
        return pos

    def tile(full, some, causal):
        f_at, s_at = (pl.ds(*full), pl.ds(*some))
        f_1, f_2, s_1, s_2 = (full_1[f_at, :], full_2[f_at, :], some_1[s_at, :], some_2[s_at, :])
        scores = lax.dot_general(f_1, s_1, nt, preferred_element_type=F32)
        shifted = lax.dot_general(f_2, s_2, nt, preferred_element_type=F32)
        probs = jnp.exp2(scores * factor)
        if causal:
            f_pos = iota((full[1], some[1]), 0) + full[0]
            s_pos = some_pos(*some)
            probs = jnp.where(f_pos <= s_pos if kind == 0 else f_pos >= s_pos, probs, 0.0)
        grads = (probs * shifted).astype(BF16)
        probs = probs.astype(BF16)
        to_full = jnp.dot(grads, s_1, preferred_element_type=F32)
        to_some = lax.dot_general(grads, f_1, tn, preferred_element_type=F32)
        if kind == 0:
            value = jnp.dot(probs, s_2[:, 0:LANES], preferred_element_type=F32)
        else:
            value = lax.dot_general(probs, f_2[:, 0:LANES], tn, preferred_element_type=F32)
        return to_full, to_some, value

    if members == 2:
        quarter = own_rows // 2
        written = set()

        def store(acc, begin, value):
            for first in range(0, value.shape[0], quarter):
                at = pl.ds(begin + first, quarter)
                part = value[first : first + quarter]
                key = (id(acc), begin + first)
                acc[at, :] = acc[at, :] + part if key in written else part
                written.add(key)

        def add(full, some, causal):
            to_full, to_some, value = tile(full, some, causal)
            store(full_acc, full[0], to_full)
            store(some_acc, some[0], to_some)
            store(value_acc, full[0] if kind == 0 else some[0], value)

        top, bottom = ((0, full_rows // 2), (full_rows // 2, full_rows // 2))
        if kind == 0:
            add(top, (0, own_rows), True)
            add(bottom, (quarter, quarter), True)
        else:
            add(bottom, (0, own_rows), True)
            add(top, (0, quarter), True)

        @pl.when(wanted)
        def _():
            add(top, (own_rows, own_rows), False)
            add(bottom, (own_rows, own_rows), False)

        @pl.when(jnp.logical_not(wanted))
        def _():
            at = pl.ds(own_rows, own_rows)
            some_acc[at, :] = jnp.zeros((own_rows, 2 * LANES), F32)
            if kind == 1:
                value_acc[at, :] = jnp.zeros((own_rows, LANES), F32)

    else:
        full_acc[...] = jnp.zeros_like(full_acc)
        some_acc[...] = jnp.zeros_like(some_acc)
        value_acc[...] = jnp.zeros_like(value_acc)

        def add(full, some, causal):
            to_full, to_some, value = tile(full, some, causal)
            full_acc[pl.ds(*full), :] += to_full
            some_acc[pl.ds(*some), :] += to_some
            value_acc[pl.ds(*(full if kind == 0 else some)), :] += value

        @pl.loop(0, heads)
        def _(k):
            full = (pl.multiple_of(k * slot_rows, math.gcd(slot_rows, LANES)), slot_rows)
            add(full, (0, own_rows), True)

            @pl.when(wanted)
            def _():
                add(full, (own_rows, own_rows), False)

    shape = (blocks, LANES)
    target_pos = block_positions(ids, shape, 0, heads, members, 0, range(count))
    onward = (iota(square, 0) >= iota(square, 1)).astype(F32)
    (q_acc, k_acc) = (some_acc, full_acc) if kind == 0 else (full_acc, some_acc)
    later, inner = (jnp.zeros(shape, F32), jnp.zeros(shape, F32))
    for m in range(-(-max(members, 2) // 8)):
        some_q, some_k = (q_sources[8 * m : 8 * m + 8], k_sources[8 * m : 8 * m + 8])
        sums = jnp.zeros((rows, LANES), F32)
        for k in range(heads):
            for s in range(len(some_q)):
                part = q_acc[q_at(k, 8 * m + s), LANES:]
                sums = jnp.where(lane == s * heads + k, part, sums)
            for s in range(len(some_k)):
                part = k_acc[k_at(k, 8 * m + s), LANES:]
                sums = jnp.where(lane == half + s * heads + k, -part, sums)
        turned = pad_rows(sums).T
        slot_pos = jnp.maximum(
            block_positions(ids, shape, 1, heads, members, 0, some_q),
            block_positions(ids, shape, 1, heads, members, half, some_k),
        )
        later += dot_exact((slot_pos > target_pos).astype(F32), turned)
        inner += dot_exact((slot_pos == target_pos).astype(F32), turned)
    suffix = jnp.sum(later, axis=1, keepdims=True) + dot_exact(inner, onward)

    def suffix_block(src, k):
        at = slice(src * heads + k, src * heads + k + 1)
        return stack_rows(split3(suffix[at])).astype(BF16)

    gate_own[...] = suffix[0:heads]
    keep_own[...] = 1.0 / (1.0 + jnp.exp(gates[0]))

    def query_grad(k, s):
        return q_acc[q_at(k, s), 0:LANES]

    def key_grad(k, s):
        return k_acc[k_at(k, s), 0:LANES]

    def value_grad(k, s):
        return value_acc[k_at(k, s), :]

    blank = jnp.zeros((rows, LANES), BF16)
    for k in range(heads):
        dq_own[k] = query_grad(k, 0)
        dk_own[k] = key_grad(k, 0)
        dv_own[k] = value_grad(k, 0)
        sends = [(to_cross, 1, members, kind == 1)]
        sends += [(to_peer[s - 1], s, s, kind == 0) for s in range(1, members)]
        for ref, s, src, keys in sends:
            ref[k, 0:rows, :] = (key_grad(k, s) if keys else query_grad(k, s)).astype(BF16)
            ref[k, rows : 2 * rows, :] = value_grad(k, s).astype(BF16) if keys else blank
            ref[k, 2 * rows :, :] = suffix_block(src, k)
        for s in range(1, members):
            to_corner[s - 1][k] = suffix_block(members + s, k)


def combine_kernel(plan, ids, dq_ref, dk_ref, dv_ref, gate_ref, keep_ref, cross, *refs):
    rows, heads, members, scale = plan
    peers, corner, out_ref = (refs[: members - 1], refs[members - 1 : -1], refs[-1])
    for kind in (0, 1):

        @pl.when(ids[KIND] == kind)
        def _(kind=kind):
            key_from, query_from = ((peers, [cross]) if kind == 0 else ([cross], peers))
            for k in range(heads):
                dq, dk, dv = (dq_ref[k], dk_ref[k], dv_ref[k])
                extra = jnp.zeros((STAT, LANES), F32)
                for ref in query_from:
                    dq += ref[k, 0:rows, :].astype(F32)
                for ref in key_from:
                    dk += ref[k, 0:rows, :].astype(F32)
                    dv += ref[k, rows : 2 * rows, :].astype(F32)
                for ref in (cross, *peers):
                    extra += ref[k, 2 * rows :, :].astype(F32)
                for ref in corner:
                    extra += ref[k].astype(F32)
                out_ref[k, 0:rows, :] = (scale * dq).astype(BF16)
                out_ref[k, rows : 2 * rows, :] = (scale * dk).astype(BF16)
                out_ref[k, 2 * rows : 3 * rows, :] = dv.astype(BF16)
                total = gate_ref[k : k + 1, :] + jnp.sum(extra, axis=0, keepdims=True)
                gate = total * keep_ref[k : k + 1, :]
                out_ref[k, 3 * rows :, :] = jnp.broadcast_to(gate, (STAT, LANES)).astype(BF16)


def unpack_kernel(in_ref, dq_ref, dk_ref, dv_ref, gate_ref):
    rows = dq_ref.shape[0]
    heads = in_ref.shape[0]
    gates = []
    for h in range(heads):
        cols = pl.ds(h * LANES, LANES)
        dq_ref[:, cols] = in_ref[h, 0:rows, :]
        dk_ref[:, cols] = in_ref[h, rows : 2 * rows, :]
        dv_ref[:, cols] = in_ref[h, 2 * rows : 3 * rows, :]
        gates.append(in_ref[h, 3 * rows :, :].astype(F32)[0:1])
    gate_ref[...] = jnp.concatenate(gates, axis=0)[:, 0:rows].astype(BF16)


def struct(shape, dtype=BF16):
    return jax.ShapeDtypeStruct(shape, dtype)


def call(kernel, out_shape, inputs, scratch=(), smem=0, space=VMEM, limit=40):
    return pl.pallas_call(
        kernel,
        out_shape=out_shape,
        in_specs=[SMEM] * smem + [space] * (len(inputs) - smem),
        out_specs=jax.tree.map(lambda _: VMEM, out_shape),
        scratch_shapes=list(scratch),
        compiler_params=pltpu.CompilerParams(vmem_limit_bytes=limit * 1024 * 1024),
    )(*inputs)


def per_device(queries, key_inputs, value_inputs, out_grad, attn_output, gate_logits, lse):
    ctx, group = (lax.axis_size("ctx"), lax.axis_size("head"))
    rows, heads = gate_logits.shape
    width = queries.shape[1]
    scale = (width // heads) ** -0.5
    half = ctx * group // 2
    members = half // heads
    both = ("ctx", "head")

    def device(side, slot, member):
        return side * half + slot * members + member

    def shift(array, across, along, chosen):
        pairs = [
            (device(side ^ across, slot, (member + along) % members), device(side, slot, member))
            for side in (0, 1)
            for slot in range(heads)
            for member in range(members)
            if chosen(side, int(slot >= heads // 2))
        ]
        return lax.ppermute(array, both, pairs)

    def everyone(side, kind):
        return True

    def working(side, kind):
        return side == kind

    def waiting(side, kind):
        return side != kind

    regions = [
        [device(side, slot, member) for slot in range(heads)] for side in (0, 1) for member in range(members)
    ]

    def exchange(array):
        return lax.all_to_all(
            array, both, split_axis=0, concat_axis=0, axis_index_groups=regions, tiled=True
        )

    here = lax.axis_index("ctx") * group + lax.axis_index("head")
    side, place = (here // half, here % half)
    slot, member = (place // members, place % members)
    kind = jnp.where(slot >= heads // 2, 1, 0)
    ids = [kind, side, member]
    for other in (0, 1):
        ids += [((side + other) % 2) * half + (member + s) % members for s in range(members)]
    ids = jnp.stack(ids).astype(jnp.int32)

    packed = call(
        pack_kernel,
        struct((heads, 4 * rows + STAT, LANES)),
        (queries, key_inputs, value_inputs, out_grad, attn_output, gate_logits.T, lse.T),
        scratch=[pltpu.VMEM((rows, width), BF16)] * 5
        + [pltpu.VMEM((heads, rows), BF16), pltpu.VMEM((heads, rows), F32)]
        + [pltpu.VMEM((heads, LANES), F32)] * 2
        + [pltpu.SemaphoreType.DMA((7,))],
        space=HBM,
        limit=PACK_LIMIT,
    )
    own = exchange(packed)
    length = 2 * rows + STAT

    def part(keys):
        return lax.dynamic_slice_in_dim(own, jnp.where(keys, 2 * rows, 0), length, axis=1)

    cross_send, peer_send = (part(kind == 1), part(kind == 0))
    stat_send = own[:, 2 * rows : length]
    cross = shift(cross_send, 1, 0, working)
    peers = [shift(peer_send, 0, s, everyone) for s in range(1, members)]
    corner = [shift(stat_send, 1, s, working) for s in range(1, members)]

    plan = (rows, heads, members, scale)
    own_rows, full_rows = (heads * rows, heads * members * rows)
    piece = struct((heads, rows, LANES), F32)
    small = struct((heads, LANES), F32)
    sent = struct((heads, length, LANES))
    dq, dk, dv, gate, keep, to_cross, *others = call(
        functools.partial(attention_kernel, plan),
        [piece, piece, piece, small, small, sent]
        + [sent] * (members - 1)
        + [struct((heads, STAT, LANES))] * (members - 1),
        (ids, own, *peers, cross, *corner),
        scratch=[
            pltpu.VMEM((full_rows, 2 * LANES), BF16),
            pltpu.VMEM((full_rows, 2 * LANES), BF16),
            pltpu.VMEM((2 * own_rows, 2 * LANES), BF16),
            pltpu.VMEM((2 * own_rows, 2 * LANES), BF16),
            pltpu.VMEM((full_rows, 2 * LANES), F32),
            pltpu.VMEM((2 * own_rows, 2 * LANES), F32),
            pltpu.VMEM((max(full_rows, 2 * own_rows), LANES), F32),
        ],
        smem=1,
    )
    to_peer, to_corner = (others[: members - 1], others[members - 1 :])
    cross = shift(to_cross, 1, 0, waiting)
    peers = [shift(to_peer[s - 1], 0, members - s, everyone) for s in range(1, members)]
    corner = [shift(to_corner[s - 1], 1, members - s, waiting) for s in range(1, members)]
    summed = call(
        functools.partial(combine_kernel, plan),
        struct((heads, 3 * rows + STAT, LANES)),
        (ids, dq, dk, dv, gate, keep, cross, *peers, *corner),
        smem=1,
    )
    final = exchange(summed)
    full = struct(queries.shape)
    dq, dk, dv, gate_grad = call(unpack_kernel, [full, full, full, struct((heads, rows))], (final,))
    return dq, dk, dv, gate_grad.T


def solution(mesh):
    split = P(("ctx", "head"), None)
    return jax.shard_map(
        per_device,
        mesh=mesh,
        in_specs=(split,) * 7,
        out_specs=(split,) * 4,
        check_vma=False,
    )
```

```python
import functools
import math

import jax
import jax.numpy as jnp
from jax import lax
from jax.experimental import pallas as pl
from jax.experimental.pallas import tpu as pltpu
from jax.sharding import PartitionSpec as P

BF16 = jnp.bfloat16
F32 = jnp.float32
LANES = 128
STAT = 16
EXACT = lax.Precision.HIGHEST
VMEM = pl.BlockSpec(memory_space=pltpu.VMEM)
HBM = pl.BlockSpec(memory_space=pltpu.HBM)
PACK_LIMIT = 64


def iota(shape, dim):
    return lax.broadcasted_iota(jnp.int32, shape, dim)


def dot_exact(a, b):
    return jnp.dot(a, b, precision=EXACT, preferred_element_type=F32)


def split3(x):
    hi = x.astype(BF16).astype(F32)
    rest = x - hi
    mid = rest.astype(BF16).astype(F32)
    low = (rest - mid).astype(BF16).astype(F32)
    return hi, mid, low


def stack_rows(rows):
    at = iota((STAT, LANES), 0)
    block = jnp.zeros((STAT, LANES), F32)
    for j, row in enumerate(rows):
        block = jnp.where(at == j, jnp.broadcast_to(row, (STAT, LANES)), block)
    return block


def pad_rows(x):
    missing = LANES - x.shape[0]
    if missing:
        x = jnp.concatenate([x, jnp.zeros((missing, x.shape[1]), x.dtype)], axis=0)
    return x


def wrap(x, n):
    return jnp.where(x >= n, x - n, x)


KIND, HALF, MEMBER, BASE = range(4)


def place_of(heads, members):
    here = lax.axis_index("ctx") * lax.axis_size("head") + lax.axis_index("head")
    half = heads * members
    side = (here >= half).astype(jnp.int32)
    place = here - side * half
    member = lax.rem(place, members)
    kind = (place >= half // 2).astype(jnp.int32)
    bases = [
        jnp.where(side == other, 0, half) + wrap(member + s, members) for other in (0, 1) for s in range(members)
    ]
    return [kind, side, member, *bases]


def block_positions(bases, shape, dim, heads, stride, first, sources):
    index = iota(shape, dim)
    pos = jnp.full(shape, -1, jnp.int32)
    for at, src in enumerate(sources):
        begin = first + at * heads
        here = (index >= begin) & (index < begin + heads)
        pos = jnp.where(here, bases[src] + (index - begin) * stride, pos)
    return pos


def pack_kernel(*refs):
    sources, out_ref, refs = (refs[:7], refs[7], refs[8:])
    heads, rows = sources[5].shape
    *held, gate_wide, lse_wide, sems = refs
    copies = [pltpu.make_async_copy(src, dst, sems.at[i]) for i, (src, dst) in enumerate(zip(sources, held))]
    for i in (5, 6, 3, 4, 0, 1, 2):
        copies[i].start()
    q_ref, k_ref, v_ref, g_ref, o_ref, gate_ref, lse_ref = held
    copies[5].wait()
    copies[6].wait()
    gate_wide[...] = jnp.zeros_like(gate_wide)
    lse_wide[...] = jnp.zeros_like(lse_wide)
    gate_wide[:, 0:rows] = gate_ref[...].astype(F32)
    lse_wide[:, 0:rows] = lse_ref[...]
    copies[3].wait()
    copies[4].wait()
    lane = iota((rows, LANES), 1)
    delta = jnp.zeros((rows, LANES), F32)
    for h in range(heads):
        cols = pl.ds(h * LANES, LANES)
        grad = g_ref[:, cols]
        row_sum = jnp.sum(grad.astype(F32) * o_ref[:, cols].astype(F32), axis=1, keepdims=True)
        delta = jnp.where(lane == h, row_sum, delta)
        out_ref[h, rows : 2 * rows, :] = grad
    parts = [gate_wide[...], *split3(lse_wide[...]), *split3(pad_rows(delta).T[:heads])]
    for h in range(heads):
        block = stack_rows([part[h : h + 1] for part in parts])
        out_ref[h, 2 * rows : 2 * rows + STAT, :] = block.astype(BF16)
    for i, ref, first in ((0, q_ref, 0), (1, k_ref, 2 * rows + STAT), (2, v_ref, 3 * rows + STAT)):
        copies[i].wait()
        for h in range(heads):
            out_ref[h, first : first + rows, :] = ref[:, pl.ds(h * LANES, LANES)]


def stat_row(block, j):
    return jnp.concatenate([block[k, j : j + 1, :].astype(F32) for k in range(block.shape[0])], axis=0)


def curves(gates, rows, members, bases):
    heads = gates[0].shape[0]
    in_row = iota((heads, LANES), 1) < rows
    logs = [
        jnp.where(in_row, jnp.minimum(x, 0.0) - jnp.log1p(jnp.exp(-jnp.abs(x))), 0.0) for x in gates
    ]
    logs = jnp.concatenate(logs, axis=0)
    square = (LANES, LANES)
    upto = (iota(square, 0) <= iota(square, 1)).astype(F32)
    shape = (members * heads, members * heads)
    row_pos = block_positions(bases, shape, 0, heads, members, 0, range(members))
    lane_pos = block_positions(bases, shape, 1, heads, members, 0, range(members))
    before = jnp.sum(dot_exact((lane_pos < row_pos).astype(F32), logs), axis=1, keepdims=True)
    curve = dot_exact(logs, upto) + before
    return [curve[s * heads : (s + 1) * heads] for s in range(members)], jnp.sum(logs)


def extra_columns(rows, scale, queries, keys):
    heads = (queries or keys)[0][0].shape[0]
    zero = jnp.zeros((heads, LANES), F32)
    score_cols, delta_cols = [], []
    for m in range(-(-max(len(queries), len(keys)) // 2)):
        q_rows, d_rows, k_rows = [], [], []
        for s in (2 * m, 2 * m + 1):
            if s < len(queries):
                curve, block = queries[s]
                lse = stat_row(block, 1) + stat_row(block, 2) + stat_row(block, 3)
                q_rows += [*split3((curve - lse) / scale), zero]
                d_rows += [-stat_row(block, 4), -stat_row(block, 5), -stat_row(block, 6), zero]
            else:
                q_rows += [zero] * 4
                d_rows += [zero] * 4
            k_rows += [*split3(-keys[s][0] / scale), zero] if s < len(keys) else [zero] * 4
        score_cols.append(jnp.concatenate(q_rows + k_rows, axis=0).T[:rows])
        if queries:
            delta_cols.append(pad_rows(jnp.concatenate(d_rows, axis=0)).T[:rows])
    return score_cols, delta_cols


def lay_out(rows, heads, columns, sides):
    score_cols, delta_cols = columns
    lane = iota((rows, LANES), 1)
    half = 8 * heads
    upper = (lane >= half).astype(F32)
    lower = (lane < half).astype(F32)
    ones = jnp.ones((rows, LANES), BF16)
    for query, sources, place, first, second in sides:
        for k in range(heads):
            for s, (array, begin) in enumerate(sources):
                at = place(k, s)
                inner = lane - (s % 2) * 4 * heads - (0 if query else half)
                mine = (inner >= 0) & (inner < 4 * heads) & (lane % heads == k)
                score = jnp.where(mine, score_cols[s // 2], upper if query else lower)
                first[at, 0:LANES] = array[k, begin : begin + rows, :]
                first[at, LANES:] = score.astype(BF16)
                second[at, 0:LANES] = array[k, begin + rows : begin + 2 * rows, :]
                if query:
                    second[at, LANES:] = jnp.where(mine, delta_cols[s // 2], 0.0).astype(BF16)
                else:
                    second[at, LANES:] = ones


def tile(scale, key, value, query, grad, allowed):
    nt = (((1,), (1,)), ((), ()))
    tn = (((0,), (0,)), ((), ()))
    scores = lax.dot_general(key, query, nt, preferred_element_type=F32)
    shifted = lax.dot_general(value, grad, nt, preferred_element_type=F32)
    probs = jnp.exp2(scores * (scale * math.log2(math.e)))
    if allowed is not None:
        probs = jnp.where(allowed, probs, 0.0)
    grads = (probs * shifted).astype(BF16)
    dk = jnp.dot(grads, query, preferred_element_type=F32)
    dq = lax.dot_general(grads, key, tn, preferred_element_type=F32)
    dv = jnp.dot(probs.astype(BF16), grad[:, 0:LANES], preferred_element_type=F32)
    return dk, dq, dv


class Sums:
    def __init__(self, ref, step, start=None):
        self.ref, self.step, self.start, self.seen = ref, step, start, set()

    def add(self, begin, value):
        for first in range(0, value.shape[0], self.step):
            at = pl.ds(begin + first, self.step)
            part = value[first : first + self.step]
            if begin + first in self.seen:
                part = self.ref[at, :] + part
            elif self.start is not None:
                part = self.start[at, :] + part
            self.ref[at, :] = part
            self.seen.add(begin + first)


def full_place(place, rows, members):
    def at(k, s):
        begin = (k * members + wrap(place[MEMBER] + s, members)) * rows
        return pl.ds(pl.multiple_of(begin, math.gcd(rows, LANES)), rows)

    return at


def some_place(rows):
    return lambda k, s: pl.ds(k * rows, rows)


def own_kernel(plan, own_ref, *refs):
    rows, heads, members, scale = plan
    peers, outs, scratch = (refs[: members - 1], refs[members - 1 : members + 5], refs[members + 5 :])
    place = place_of(heads, members)
    for kind in (0, 1):

        @pl.when(place[KIND] == kind)
        def _(kind=kind):
            own_body(plan, kind, place, own_ref, peers, outs, scratch)


def own_body(plan, kind, place, own_ref, peers, outs, scratch):
    rows, heads, members, scale = plan
    full_1, full_2, full_acc, some_acc, value_acc, total_ref = outs
    some_1, some_2 = scratch
    stat_at = 2 * rows
    peer_stat = 0 if kind == 0 else stat_at
    blocks = [own_ref[:, stat_at : stat_at + STAT, :].astype(F32)]
    blocks += [ref[:, peer_stat : peer_stat + STAT, :].astype(F32) for ref in peers]
    curve, total = curves([stat_row(block, 0) for block in blocks], rows, members, place[BASE:])
    total_ref[...] = jnp.full(total_ref.shape, total, F32)
    every = list(zip(curve, blocks))
    full_at, some_at = (full_place(place, rows, members), some_place(rows))
    keys_at = stat_at + STAT
    if kind == 0:
        columns = extra_columns(rows, scale, every[:1], every)
        query_sources = [(own_ref, 0)]
        key_sources = [(own_ref, keys_at)] + [(ref, STAT) for ref in peers]
        (k_1, k_2, k_acc, k_at), (q_1, q_2, q_acc, q_at) = (
            (full_1, full_2, full_acc, full_at),
            (some_1, some_2, some_acc, some_at),
        )
    else:
        columns = extra_columns(rows, scale, every, every[:1])
        query_sources = [(own_ref, 0)] + [(ref, 0) for ref in peers]
        key_sources = [(own_ref, keys_at)]
        (q_1, q_2, q_acc, q_at), (k_1, k_2, k_acc, k_at) = (
            (full_1, full_2, full_acc, full_at),
            (some_1, some_2, some_acc, some_at),
        )
    sides = [(True, query_sources, q_at, q_1, q_2), (False, key_sources, k_at, k_1, k_2)]
    lay_out(rows, heads, columns, sides)
    own_rows, slot_rows = (heads * rows, members * rows)

    def full_pos(shape, dim, begin):
        return iota(shape, dim) + begin

    def some_pos(shape, dim, begin):
        index = iota(shape, dim) + begin
        pos = index + place[MEMBER] * rows
        for k in range(1, heads):
            pos = jnp.where(index >= k * rows, pos + (slot_rows - rows), pos)
        return pos

    def product(keys, queries, causal):
        allowed = None
        if causal:
            k_pos, q_pos = ((full_pos, some_pos) if kind == 0 else (some_pos, full_pos))
            allowed = k_pos((keys[1], 1), 0, keys[0]) <= q_pos((1, queries[1]), 1, queries[0])
        k_rows, q_rows = (pl.ds(*keys), pl.ds(*queries))
        return tile(scale, k_1[k_rows, :], k_2[k_rows, :], q_1[q_rows, :], q_2[q_rows, :], allowed)

    if members == 2:
        part = own_rows // 2
        sums = [Sums(k_acc, part), Sums(q_acc, part), Sums(value_acc, part)]

        def add(keys, queries, causal):
            dk, dq, dv = product(keys, queries, causal)
            sums[0].add(keys[0], dk)
            sums[1].add(queries[0], dq)
            sums[2].add(keys[0], dv)

        if kind == 0:
            for i in range(4):
                add((i * part, part), (0, own_rows) if i < 2 else (part, part), True)
        else:
            add((0, part), (0, own_rows), True)
            add((0, part), (own_rows, own_rows), False)
            add((part, part), (own_rows, own_rows), True)
    else:
        full_acc[...] = jnp.zeros_like(full_acc)
        some_acc[...] = jnp.zeros_like(some_acc)
        value_acc[...] = jnp.zeros_like(value_acc)

        @pl.loop(0, heads)
        def _(k):
            full = (pl.multiple_of(k * slot_rows, math.gcd(slot_rows, LANES)), slot_rows)
            keys, queries = ((full, (0, own_rows)) if kind == 0 else ((0, own_rows), full))
            dk, dq, dv = product(keys, queries, True)
            k_acc[pl.ds(*keys), :] += dk
            q_acc[pl.ds(*queries), :] += dq
            value_acc[pl.ds(*keys), :] += dv


def square_kernel(plan, *refs):
    rows, heads, members, scale = plan
    chunks = -(-members // 8)
    cut = 7 + members - 1
    ins, outs, scratch = (
        refs[:cut],
        refs[cut : cut + 4 + members - 1 + chunks],
        refs[cut + 4 + members - 1 + chunks :],
    )
    place = place_of(heads, members)
    for kind in (0, 1):

        @pl.when(place[KIND] == kind)
        def _(kind=kind):
            square_body(plan, kind, place, ins, outs, scratch)


def square_body(plan, kind, place, ins, outs, scratch):
    rows, heads, members, scale = plan
    full_1, full_2, full_in, some_in, value_in, total_ref, cross, *corner = ins
    dq_own, dk_own, dv_own, to_cross = outs[:4]
    to_peer, sums_refs = (outs[4 : 3 + members], outs[3 + members :])
    cross_1, cross_2, full_acc, cross_acc, value_acc = scratch
    own_rows = heads * rows
    full_rows = own_rows * members
    full_at, some_at = (full_place(place, rows, members), some_place(rows))
    wanted = place[HALF] == kind

    @pl.when(wanted)
    def _():
        stat_at = 2 * rows if kind == 0 else 0
        block = cross[:, stat_at : stat_at + STAT, :].astype(F32)
        gates = [stat_row(block, 0)] + [ref[...].astype(F32) for ref in corner]
        curve, total = curves(gates, rows, members, place[BASE + members :])
        if kind == 0:
            columns = extra_columns(rows, scale, [(curve[0] + total_ref[...], block)], [])
            side = (True, [(cross, 0)], some_at, cross_1, cross_2)
        else:
            columns = extra_columns(rows, scale, [], [(curve[0] - total, block)])
            side = (False, [(cross, STAT)], some_at, cross_1, cross_2)
        lay_out(rows, heads, columns, [side])
        if members == 2:
            part = own_rows // 2
            full_sums = Sums(full_acc, part, full_in)
            cross_sums = Sums(cross_acc, part)
            if kind == 0:
                value_sums = Sums(value_acc, part, value_in)
                for i in range(4):
                    at = pl.ds(i * part, part)
                    dk, dq, dv = tile(
                        scale, full_1[at, :], full_2[at, :], cross_1[...], cross_2[...], None
                    )
                    full_sums.add(i * part, dk)
                    cross_sums.add(0, dq)
                    value_sums.add(i * part, dv)
            else:
                value_acc[0:own_rows, :] = value_in[0:own_rows, :]
                value_sums = Sums(value_acc, part)
                for i in (0, 1):
                    for j in (0, 1):
                        k_rows, q_rows = (pl.ds(i * part, part), pl.ds(j * own_rows, own_rows))
                        dk, dq, dv = tile(
                            scale,
                            cross_1[k_rows, :],
                            cross_2[k_rows, :],
                            full_1[q_rows, :],
                            full_2[q_rows, :],
                            None,
                        )
                        cross_sums.add(i * part, dk)
                        full_sums.add(j * own_rows, dq)
                        value_sums.add(own_rows + i * part, dv)
        else:
            full_acc[...] = full_in[...]
            value_acc[...] = value_in[...]
            cross_acc[...] = jnp.zeros_like(cross_acc)
            if kind == 1:
                value_acc[pl.ds(own_rows, own_rows), :] = jnp.zeros((own_rows, LANES), F32)
            slot_rows = members * rows

            @pl.loop(0, heads)
            def _(k):
                at = pl.ds(pl.multiple_of(k * slot_rows, math.gcd(slot_rows, LANES)), slot_rows)
                if kind == 0:
                    dk, dq, dv = tile(
                        scale, full_1[at, :], full_2[at, :], cross_1[...], cross_2[...], None
                    )
                    full_acc[at, :] += dk
                    cross_acc[...] += dq
                    value_acc[at, :] += dv
                else:
                    dk, dq, dv = tile(
                        scale, cross_1[...], cross_2[...], full_1[at, :], full_2[at, :], None
                    )
                    cross_acc[...] += dk
                    full_acc[at, :] += dq
                    value_acc[pl.ds(own_rows, own_rows), :] += dv

    @pl.when(jnp.logical_not(wanted))
    def _():
        full_acc[...] = full_in[...]
        cross_acc[...] = jnp.zeros_like(cross_acc)
        value_acc[...] = value_in[...]
        if kind == 1:
            value_acc[pl.ds(own_rows, own_rows), :] = jnp.zeros((own_rows, LANES), F32)

    def some_ref(s):
        return some_in if s == 0 else cross_acc

    def full_grad(k, s, lanes):
        return full_acc[full_at(k, s), lanes]

    def some_grad(k, s, lanes):
        return some_ref(s)[some_at(k, s), lanes]

    (query_grad, key_grad) = (some_grad, full_grad) if kind == 0 else (full_grad, some_grad)
    query_count, key_count = ((2, members) if kind == 0 else (members, 2))
    low, high = (slice(0, LANES), slice(LANES, 2 * LANES))

    def value_grad(k, s):
        if kind == 0:
            return value_acc[full_at(k, s), :]
        return value_acc[pl.ds((s * heads + k) * rows, rows), :]

    lane = iota((rows, LANES), 1)
    half = 8 * heads
    for m, sums_ref in enumerate(sums_refs):
        sums = jnp.zeros((rows, LANES), F32)
        for k in range(heads):
            for s in range(8 * m, min(8 * m + 8, query_count)):
                at = (s - 8 * m) * heads + k
                sums = jnp.where(lane == at, query_grad(k, s, high), sums)
            for s in range(8 * m, min(8 * m + 8, key_count)):
                at = half + (s - 8 * m) * heads + k
                sums = jnp.where(lane == at, -key_grad(k, s, high), sums)
        sums_ref[...] = sums
    blank = jnp.zeros((rows, LANES), BF16)
    for k in range(heads):
        dq_own[k] = query_grad(k, 0, low)
        dk_own[k] = key_grad(k, 0, low)
        dv_own[k] = value_grad(k, 0)
        sends = [(to_cross, 1, kind == 1)]
        sends += [(to_peer[s - 1], s, kind == 0) for s in range(1, members)]
        for ref, s, keys in sends:
            ref[k, 0:rows, :] = (key_grad(k, s, low) if keys else query_grad(k, s, low)).astype(BF16)
            ref[k, rows : 2 * rows, :] = value_grad(k, s).astype(BF16) if keys else blank


def suffix_kernel(plan, *refs):
    rows, heads, members, scale = plan
    chunks = -(-members // 8)
    sums_refs, outs = (refs[:chunks], refs[chunks:])
    place = place_of(heads, members)
    bases = place[BASE:]
    first_kind = place[KIND] == 0
    count = 2 * members
    half = 8 * heads
    square = (LANES, LANES)
    shape = (count * heads, LANES)
    target_pos = block_positions(bases, shape, 0, heads, members, 0, range(count))
    onward = (iota(square, 0) >= iota(square, 1)).astype(F32)
    later, inner = (jnp.zeros(shape, F32), jnp.zeros(shape, F32))
    pair = [0, members]
    for m, sums_ref in enumerate(sums_refs):
        turned = pad_rows(sums_ref[...]).T
        some = pair if m == 0 else []
        full = range(8 * m, min(8 * m + 8, members))
        slot_pos = [
            jnp.maximum(
                block_positions(bases, (8, LANES), 1, heads, members, 0, queries),
                block_positions(bases, (8, LANES), 1, heads, members, half, keys),
            )[0:1]
            for queries, keys in ((some, full), (full, some))
        ]
        slot_pos = jnp.where(first_kind, slot_pos[0], slot_pos[1])
        later += dot_exact((slot_pos > target_pos).astype(F32), turned)
        inner += dot_exact((slot_pos == target_pos).astype(F32), turned)
    suffix = jnp.sum(later, axis=1, keepdims=True) + dot_exact(inner, onward)
    for src, ref in enumerate(outs):
        ref[...] = suffix[src * heads : (src + 1) * heads]


def combine_kernel(plan, dq_ref, dk_ref, dv_ref, cross, *refs):
    rows, heads, members, scale = plan
    peers, gate_refs, out_ref = (refs[: members - 1], refs[members - 1 : -1], refs[-1])
    first_kind = place_of(heads, members)[KIND] == 0
    gates = gate_refs[0][...]
    for ref in gate_refs[1:]:
        gates += ref[...]
    gates = split3(gates)
    for k in range(heads):
        far = cross[k].astype(F32)
        near = peers[0][k].astype(F32)
        for ref in peers[1:]:
            near += ref[k].astype(F32)
        to_keys = jnp.where(first_kind, near, far)
        to_queries = jnp.where(first_kind, far[0:rows], near[0:rows])
        out_ref[k, 0:rows, :] = (scale * (dq_ref[k] + to_queries)).astype(BF16)
        out_ref[k, rows : 2 * rows, :] = (scale * (dk_ref[k] + to_keys[0:rows])).astype(BF16)
        out_ref[k, 2 * rows : 3 * rows, :] = (dv_ref[k] + to_keys[rows:]).astype(BF16)
        out_ref[k, 3 * rows :, :] = stack_rows([part[k : k + 1] for part in gates]).astype(BF16)


def unpack_kernel(in_ref, keep_ref, dq_ref, dk_ref, dv_ref, gate_ref):
    rows = dq_ref.shape[0]
    heads = in_ref.shape[0]
    gates = []
    for h in range(heads):
        cols = pl.ds(h * LANES, LANES)
        dq_ref[:, cols] = in_ref[h, 0:rows, :]
        dk_ref[:, cols] = in_ref[h, rows : 2 * rows, :]
        dv_ref[:, cols] = in_ref[h, 2 * rows : 3 * rows, :]
        gates.append(jnp.sum(in_ref[h, 3 * rows :, :].astype(F32), axis=0, keepdims=True))
    gate_ref[...] = (jnp.concatenate(gates, axis=0)[:, 0:rows] * keep_ref[...]).astype(BF16)


def struct(shape, dtype=BF16):
    return jax.ShapeDtypeStruct(shape, dtype)


def call(kernel, out_shape, inputs, scratch=(), space=VMEM, limit=40):
    return pl.pallas_call(
        kernel,
        out_shape=out_shape,
        in_specs=[space] * len(inputs),
        out_specs=jax.tree.map(lambda _: VMEM, out_shape),
        scratch_shapes=list(scratch),
        compiler_params=pltpu.CompilerParams(vmem_limit_bytes=int(limit * 1024 * 1024)),
    )(*inputs)


def per_device(queries, key_inputs, value_inputs, out_grad, attn_output, gate_logits, lse):
    ctx, group = (lax.axis_size("ctx"), lax.axis_size("head"))
    rows, heads = gate_logits.shape
    width = queries.shape[1]
    scale = (width // heads) ** -0.5
    half = ctx * group // 2
    members = half // heads
    both = ("ctx", "head")

    def device(side, slot, member):
        return side * half + slot * members + member

    def shift(array, across, along, chosen):
        pairs = [
            (device(side ^ across, slot, (member + along) % members), device(side, slot, member))
            for side in (0, 1)
            for slot in range(heads)
            for member in range(members)
            if chosen(side, int(slot >= heads // 2))
        ]
        return lax.ppermute(array, both, pairs)

    def everyone(side, kind):
        return True

    def working(side, kind):
        return side == kind

    def waiting(side, kind):
        return side != kind

    regions = [
        [device(side, slot, member) for slot in range(heads)] for side in (0, 1) for member in range(members)
    ]

    def exchange(array):
        return lax.all_to_all(
            array, both, split_axis=0, concat_axis=0, axis_index_groups=regions, tiled=True
        )

    kind = place_of(heads, members)[KIND]

    packed = call(
        pack_kernel,
        struct((heads, 4 * rows + STAT, LANES)),
        (queries, key_inputs, value_inputs, out_grad, attn_output, gate_logits.T, lse.T),
        scratch=[pltpu.VMEM((rows, width), BF16)] * 5
        + [pltpu.VMEM((heads, rows), BF16), pltpu.VMEM((heads, rows), F32)]
        + [pltpu.VMEM((heads, LANES), F32)] * 2
        + [pltpu.SemaphoreType.DMA((7,))],
        space=HBM,
        limit=PACK_LIMIT,
    )
    own = exchange(packed)
    length = 2 * rows + STAT

    def part(keys):
        return lax.dynamic_slice_in_dim(own, jnp.where(keys, 2 * rows, 0), length, axis=1)

    cross_send, peer_send = (part(kind == 1), part(kind == 0))
    gate_send = own[:, 2 * rows]
    cross = shift(cross_send, 1, 0, working)
    peers = [shift(peer_send, 0, s, everyone) for s in range(1, members)]
    corner = [shift(gate_send, 1, s, working) for s in range(1, members)]

    plan = (rows, heads, members, scale)
    own_rows, full_rows = (heads * rows, heads * members * rows)
    value_rows = max(full_rows, 2 * own_rows)
    wide = 2 * LANES
    small = struct((heads, LANES), F32)
    state = call(
        functools.partial(own_kernel, plan),
        [
            struct((full_rows, wide)),
            struct((full_rows, wide)),
            struct((full_rows, wide), F32),
            struct((own_rows, wide), F32),
            struct((value_rows, LANES), F32),
            small,
        ],
        (own, *peers),
        scratch=[pltpu.VMEM((own_rows, wide), BF16)] * 2,
    )
    piece = struct((heads, rows, LANES), F32)
    sent = struct((heads, 2 * rows, LANES))
    chunks = -(-members // 8)
    dq, dk, dv, to_cross, *others = call(
        functools.partial(square_kernel, plan),
        [piece, piece, piece, sent] + [sent] * (members - 1) + [struct((rows, LANES), F32)] * chunks,
        (*state, cross, *corner),
        scratch=[pltpu.VMEM((own_rows, wide), BF16)] * 2
        + [
            pltpu.VMEM((full_rows, wide), F32),
            pltpu.VMEM((own_rows, wide), F32),
            pltpu.VMEM((value_rows, LANES), F32),
        ],
    )
    to_peer, sums = (others[: members - 1], others[members - 1 :])
    cross = shift(to_cross, 1, 0, waiting)
    peers = [shift(to_peer[s - 1], 0, members - s, everyone) for s in range(1, members)]
    gates = call(functools.partial(suffix_kernel, plan), [small] * (2 * members), tuple(sums))
    gates = (
        [gates[0]]
        + [shift(gates[s], 0, members - s, everyone) for s in range(1, members)]
        + [shift(gates[members + s], 1, (members - s) % members, waiting) for s in range(members)]
    )
    summed = call(
        functools.partial(combine_kernel, plan),
        struct((heads, 3 * rows + STAT, LANES)),
        (dq, dk, dv, cross, *peers, *gates),
    )
    final = exchange(summed)
    keep = jax.nn.sigmoid(-gate_logits.T.astype(F32))
    full = struct(queries.shape)
    dq, dk, dv, gate_grad = call(unpack_kernel, [full, full, full, struct((heads, rows))], (final, keep))
    return dq, dk, dv, gate_grad.T


def solution(mesh):
    split = P(("ctx", "head"), None)
    return jax.shard_map(
        per_device,
        mesh=mesh,
        in_specs=(split,) * 7,
        out_specs=(split,) * 4,
        check_vma=False,
    )
```

```python
import functools
import math

import jax
import jax.numpy as jnp
from jax import lax
from jax.experimental import pallas as pl
from jax.experimental.pallas import tpu as pltpu
from jax.sharding import PartitionSpec as P

BF16 = jnp.bfloat16
F32 = jnp.float32
LANES = 128
STAT = 16
EXACT = lax.Precision.HIGHEST
VMEM = pl.BlockSpec(memory_space=pltpu.VMEM)
HBM = pl.BlockSpec(memory_space=pltpu.HBM)
PACK_LIMIT = 64


def iota(shape, dim):
    return lax.broadcasted_iota(jnp.int32, shape, dim)


def dot_exact(a, b):
    return jnp.dot(a, b, precision=EXACT, preferred_element_type=F32)


def split3(x):
    hi = x.astype(BF16).astype(F32)
    rest = x - hi
    mid = rest.astype(BF16).astype(F32)
    low = (rest - mid).astype(BF16).astype(F32)
    return hi, mid, low


def stack_rows(rows):
    at = iota((STAT, LANES), 0)
    block = jnp.zeros((STAT, LANES), F32)
    for j, row in enumerate(rows):
        block = jnp.where(at == j, jnp.broadcast_to(row, (STAT, LANES)), block)
    return block


def pad_rows(x):
    missing = LANES - x.shape[0]
    if missing:
        x = jnp.concatenate([x, jnp.zeros((missing, x.shape[1]), x.dtype)], axis=0)
    return x


def wrap(x, n):
    return jnp.where(x >= n, x - n, x)


KIND, HALF, MEMBER, BASE = range(4)


def place_of(heads, members):
    here = lax.axis_index("ctx") * lax.axis_size("head") + lax.axis_index("head")
    half = heads * members
    side = (here >= half).astype(jnp.int32)
    place = here - side * half
    member = lax.rem(place, members)
    kind = (place >= half // 2).astype(jnp.int32)
    bases = [
        jnp.where(side == other, 0, half) + wrap(member + s, members) for other in (0, 1) for s in range(members)
    ]
    return [kind, side, member, *bases]


def block_positions(bases, shape, dim, heads, stride, first, sources):
    index = iota(shape, dim)
    pos = jnp.full(shape, -1, jnp.int32)
    for at, src in enumerate(sources):
        begin = first + at * heads
        here = (index >= begin) & (index < begin + heads)
        pos = jnp.where(here, bases[src] + (index - begin) * stride, pos)
    return pos


def pack_kernel(*refs):
    sources, out_ref, refs = (refs[:7], refs[7], refs[8:])
    heads, rows = sources[5].shape
    *held, gate_wide, lse_wide, sems = refs
    copies = [pltpu.make_async_copy(src, dst, sems.at[i]) for i, (src, dst) in enumerate(zip(sources, held))]
    for i in (5, 6, 3, 4, 0, 1, 2):
        copies[i].start()
    q_ref, k_ref, v_ref, g_ref, o_ref, gate_ref, lse_ref = held
    copies[5].wait()
    copies[6].wait()
    gate_wide[...] = jnp.zeros_like(gate_wide)
    lse_wide[...] = jnp.zeros_like(lse_wide)
    gate_wide[:, 0:rows] = gate_ref[...].astype(F32)
    lse_wide[:, 0:rows] = lse_ref[...]
    copies[3].wait()
    copies[4].wait()
    lane = iota((rows, LANES), 1)
    delta = jnp.zeros((rows, LANES), F32)
    for h in range(heads):
        cols = pl.ds(h * LANES, LANES)
        grad = g_ref[:, cols]
        row_sum = jnp.sum(grad.astype(F32) * o_ref[:, cols].astype(F32), axis=1, keepdims=True)
        delta = jnp.where(lane == h, row_sum, delta)
        out_ref[h, rows : 2 * rows, :] = grad
    parts = [gate_wide[...], *split3(lse_wide[...]), *split3(pad_rows(delta).T[:heads])]
    for h in range(heads):
        block = stack_rows([part[h : h + 1] for part in parts])
        out_ref[h, 2 * rows : 2 * rows + STAT, :] = block.astype(BF16)
    for i, ref, first in ((0, q_ref, 0), (1, k_ref, 2 * rows + STAT), (2, v_ref, 3 * rows + STAT)):
        copies[i].wait()
        for h in range(heads):
            out_ref[h, first : first + rows, :] = ref[:, pl.ds(h * LANES, LANES)]


def stat_row(block, j):
    return jnp.concatenate([block[k, j : j + 1, :].astype(F32) for k in range(block.shape[0])], axis=0)


def curves(gates, rows, members, bases):
    heads = gates[0].shape[0]
    in_row = iota((heads, LANES), 1) < rows
    logs = [
        jnp.where(in_row, jnp.minimum(x, 0.0) - jnp.log1p(jnp.exp(-jnp.abs(x))), 0.0) for x in gates
    ]
    logs = jnp.concatenate(logs, axis=0)
    square = (LANES, LANES)
    upto = (iota(square, 0) <= iota(square, 1)).astype(F32)
    shape = (members * heads, members * heads)
    row_pos = block_positions(bases, shape, 0, heads, members, 0, range(members))
    lane_pos = block_positions(bases, shape, 1, heads, members, 0, range(members))
    before = jnp.sum(dot_exact((lane_pos < row_pos).astype(F32), logs), axis=1, keepdims=True)
    curve = dot_exact(logs, upto) + before
    return [curve[s * heads : (s + 1) * heads] for s in range(members)], jnp.sum(logs)


def extra_columns(rows, scale, queries, keys):
    heads = (queries or keys)[0][0].shape[0]
    zero = jnp.zeros((heads, LANES), F32)
    score_cols, delta_cols = [], []
    for m in range(-(-max(len(queries), len(keys)) // 2)):
        q_rows, d_rows, k_rows = [], [], []
        for s in (2 * m, 2 * m + 1):
            if s < len(queries):
                curve, block = queries[s]
                lse = stat_row(block, 1) + stat_row(block, 2) + stat_row(block, 3)
                q_rows += [*split3((curve - lse) / scale), zero]
                d_rows += [-stat_row(block, 4), -stat_row(block, 5), -stat_row(block, 6), zero]
            else:
                q_rows += [zero] * 4
                d_rows += [zero] * 4
            k_rows += [*split3(-keys[s][0] / scale), zero] if s < len(keys) else [zero] * 4
        score_cols.append(jnp.concatenate(q_rows + k_rows, axis=0).T[:rows])
        if queries:
            delta_cols.append(pad_rows(jnp.concatenate(d_rows, axis=0)).T[:rows])
    return score_cols, delta_cols


def lay_out(rows, heads, columns, sides):
    score_cols, delta_cols = columns
    lane = iota((rows, LANES), 1)
    half = 8 * heads
    upper = (lane >= half).astype(F32)
    lower = (lane < half).astype(F32)
    ones = jnp.ones((rows, LANES), BF16)
    for query, sources, place, first, second in sides:
        for k in range(heads):
            for s, (array, begin) in enumerate(sources):
                at = place(k, s)
                inner = lane - (s % 2) * 4 * heads - (0 if query else half)
                mine = (inner >= 0) & (inner < 4 * heads) & (lane % heads == k)
                score = jnp.where(mine, score_cols[s // 2], upper if query else lower)
                first[at, 0:LANES] = array[k, begin : begin + rows, :]
                first[at, LANES:] = score.astype(BF16)
                second[at, 0:LANES] = array[k, begin + rows : begin + 2 * rows, :]
                if query:
                    second[at, LANES:] = jnp.where(mine, delta_cols[s // 2], 0.0).astype(BF16)
                else:
                    second[at, LANES:] = ones


def tile(scale, key, value, query, grad, allowed):
    nt = (((1,), (1,)), ((), ()))
    tn = (((0,), (0,)), ((), ()))
    scores = lax.dot_general(key, query, nt, preferred_element_type=F32)
    shifted = lax.dot_general(value, grad, nt, preferred_element_type=F32)
    probs = jnp.exp2(scores * (scale * math.log2(math.e)))
    if allowed is not None:
        probs = jnp.where(allowed, probs, 0.0)
    grads = (probs * shifted).astype(BF16)
    dk = jnp.dot(grads, query, preferred_element_type=F32)
    dq = lax.dot_general(grads, key, tn, preferred_element_type=F32)
    dv = jnp.dot(probs.astype(BF16), grad[:, 0:LANES], preferred_element_type=F32)
    return dk, dq, dv


class Sums:
    def __init__(self, ref, step, start=None):
        self.ref, self.step, self.start, self.seen = ref, step, start, set()

    def add(self, begin, value):
        for first in range(0, value.shape[0], self.step):
            at = pl.ds(begin + first, self.step)
            part = value[first : first + self.step]
            if begin + first in self.seen:
                part = self.ref[at, :] + part
            elif self.start is not None:
                part = self.start[at, :] + part
            self.ref[at, :] = part
            self.seen.add(begin + first)


def full_place(place, rows, members):
    def at(k, s):
        begin = (k * members + wrap(place[MEMBER] + s, members)) * rows
        return pl.ds(pl.multiple_of(begin, math.gcd(rows, LANES)), rows)

    return at


def some_place(rows):
    return lambda k, s: pl.ds(k * rows, rows)


def own_kernel(plan, own_ref, *refs):
    rows, heads, members, scale = plan
    others = members - 1
    peers, stats, refs = (refs[:others], refs[others : 2 * others], refs[2 * others :])
    place = place_of(heads, members)
    for kind in (0, 1):

        @pl.when(place[KIND] == kind)
        def _(kind=kind):
            own_body(plan, kind, place, own_ref, peers, stats, refs[:7], refs[7:])


def own_body(plan, kind, place, own_ref, peers, stats, outs, scratch):
    rows, heads, members, scale = plan
    full_1, full_2, full_acc, some_acc, value_acc, total_ref, keep_ref = outs
    some_1, some_2 = scratch
    stat_at = 2 * rows
    blocks = [own_ref[:, stat_at : stat_at + STAT, :].astype(F32)]
    blocks += [ref[...].astype(F32) for ref in stats]
    gates = [stat_row(block, 0) for block in blocks]
    curve, total = curves(gates, rows, members, place[BASE:])
    keep_ref[...] = 1.0 / (1.0 + jnp.exp(gates[0]))
    total_ref[...] = jnp.full(total_ref.shape, total, F32)
    every = list(zip(curve, blocks))
    full_at, some_at = (full_place(place, rows, members), some_place(rows))
    keys_at = stat_at + STAT
    if kind == 0:
        columns = extra_columns(rows, scale, every[:1], every)
        query_sources = [(own_ref, 0)]
        key_sources = [(own_ref, keys_at)] + [(ref, 0) for ref in peers]
        (k_1, k_2, k_acc, k_at), (q_1, q_2, q_acc, q_at) = (
            (full_1, full_2, full_acc, full_at),
            (some_1, some_2, some_acc, some_at),
        )
    else:
        columns = extra_columns(rows, scale, every, every[:1])
        query_sources = [(own_ref, 0)] + [(ref, 0) for ref in peers]
        key_sources = [(own_ref, keys_at)]
        (q_1, q_2, q_acc, q_at), (k_1, k_2, k_acc, k_at) = (
            (full_1, full_2, full_acc, full_at),
            (some_1, some_2, some_acc, some_at),
        )
    sides = [(True, query_sources, q_at, q_1, q_2), (False, key_sources, k_at, k_1, k_2)]
    lay_out(rows, heads, columns, sides)
    own_rows, slot_rows = (heads * rows, members * rows)

    def full_pos(shape, dim, begin):
        return iota(shape, dim) + begin

    def some_pos(shape, dim, begin):
        index = iota(shape, dim) + begin
        pos = index + place[MEMBER] * rows
        for k in range(1, heads):
            pos = jnp.where(index >= k * rows, pos + (slot_rows - rows), pos)
        return pos

    def product(keys, queries, causal):
        allowed = None
        if causal:
            k_pos, q_pos = ((full_pos, some_pos) if kind == 0 else (some_pos, full_pos))
            allowed = k_pos((keys[1], 1), 0, keys[0]) <= q_pos((1, queries[1]), 1, queries[0])
        k_rows, q_rows = (pl.ds(*keys), pl.ds(*queries))
        return tile(scale, k_1[k_rows, :], k_2[k_rows, :], q_1[q_rows, :], q_2[q_rows, :], allowed)

    if members == 2:
        part = own_rows // 2
        sums = [Sums(k_acc, part), Sums(q_acc, part), Sums(value_acc, part)]

        def add(keys, queries, causal):
            dk, dq, dv = product(keys, queries, causal)
            sums[0].add(keys[0], dk)
            sums[1].add(queries[0], dq)
            sums[2].add(keys[0], dv)

        if kind == 0:
            for i in range(4):
                add((i * part, part), (0, own_rows) if i < 2 else (part, part), True)
        else:
            add((0, part), (0, own_rows), True)
            add((0, part), (own_rows, own_rows), False)
            add((part, part), (own_rows, own_rows), True)
    else:
        full_acc[...] = jnp.zeros_like(full_acc)
        some_acc[...] = jnp.zeros_like(some_acc)
        value_acc[...] = jnp.zeros_like(value_acc)

        @pl.loop(0, heads)
        def _(k):
            full = (pl.multiple_of(k * slot_rows, math.gcd(slot_rows, LANES)), slot_rows)
            keys, queries = ((full, (0, own_rows)) if kind == 0 else ((0, own_rows), full))
            dk, dq, dv = product(keys, queries, True)
            k_acc[pl.ds(*keys), :] += dk
            q_acc[pl.ds(*queries), :] += dq
            value_acc[pl.ds(*keys), :] += dv


def square_kernel(plan, *refs):
    rows, heads, members, scale = plan
    chunks = -(-members // 8)
    cut = 7 + members - 1
    ins, outs, scratch = (
        refs[:cut],
        refs[cut : cut + 4 + members - 1 + chunks],
        refs[cut + 4 + members - 1 + chunks :],
    )
    place = place_of(heads, members)
    for kind in (0, 1):

        @pl.when(place[KIND] == kind)
        def _(kind=kind):
            square_body(plan, kind, place, ins, outs, scratch)


def square_body(plan, kind, place, ins, outs, scratch):
    rows, heads, members, scale = plan
    full_1, full_2, full_in, some_in, value_in, total_ref, cross, *corner = ins
    dq_own, dk_own, dv_own, to_cross = outs[:4]
    to_peer, sums_refs = (outs[4 : 3 + members], outs[3 + members :])
    cross_1, cross_2, full_acc, cross_acc, value_acc = scratch
    own_rows = heads * rows
    full_rows = own_rows * members
    full_at, some_at = (full_place(place, rows, members), some_place(rows))
    wanted = place[HALF] == kind

    @pl.when(wanted)
    def _():
        stat_at = 2 * rows if kind == 0 else 0
        block = cross[:, stat_at : stat_at + STAT, :].astype(F32)
        gates = [stat_row(block, 0)] + [ref[...].astype(F32) for ref in corner]
        curve, total = curves(gates, rows, members, place[BASE + members :])
        if kind == 0:
            columns = extra_columns(rows, scale, [(curve[0] + total_ref[...], block)], [])
            side = (True, [(cross, 0)], some_at, cross_1, cross_2)
        else:
            columns = extra_columns(rows, scale, [], [(curve[0] - total, block)])
            side = (False, [(cross, STAT)], some_at, cross_1, cross_2)
        lay_out(rows, heads, columns, [side])
        if members == 2:
            part = own_rows // 2
            full_sums = Sums(full_acc, part, full_in)
            cross_sums = Sums(cross_acc, part)
            if kind == 0:
                value_sums = Sums(value_acc, part, value_in)
                for i in range(4):
                    at = pl.ds(i * part, part)
                    dk, dq, dv = tile(
                        scale, full_1[at, :], full_2[at, :], cross_1[...], cross_2[...], None
                    )
                    full_sums.add(i * part, dk)
                    cross_sums.add(0, dq)
                    value_sums.add(i * part, dv)
            else:
                value_acc[0:own_rows, :] = value_in[0:own_rows, :]
                value_sums = Sums(value_acc, part)
                for i in (0, 1):
                    for j in (0, 1):
                        k_rows, q_rows = (pl.ds(i * part, part), pl.ds(j * own_rows, own_rows))
                        dk, dq, dv = tile(
                            scale,
                            cross_1[k_rows, :],
                            cross_2[k_rows, :],
                            full_1[q_rows, :],
                            full_2[q_rows, :],
                            None,
                        )
                        cross_sums.add(i * part, dk)
                        full_sums.add(j * own_rows, dq)
                        value_sums.add(own_rows + i * part, dv)
        else:
            full_acc[...] = full_in[...]
            value_acc[...] = value_in[...]
            cross_acc[...] = jnp.zeros_like(cross_acc)
            if kind == 1:
                value_acc[pl.ds(own_rows, own_rows), :] = jnp.zeros((own_rows, LANES), F32)
            slot_rows = members * rows

            @pl.loop(0, heads)
            def _(k):
                at = pl.ds(pl.multiple_of(k * slot_rows, math.gcd(slot_rows, LANES)), slot_rows)
                if kind == 0:
                    dk, dq, dv = tile(
                        scale, full_1[at, :], full_2[at, :], cross_1[...], cross_2[...], None
                    )
                    full_acc[at, :] += dk
                    cross_acc[...] += dq
                    value_acc[at, :] += dv
                else:
                    dk, dq, dv = tile(
                        scale, cross_1[...], cross_2[...], full_1[at, :], full_2[at, :], None
                    )
                    cross_acc[...] += dk
                    full_acc[at, :] += dq
                    value_acc[pl.ds(own_rows, own_rows), :] += dv

    @pl.when(jnp.logical_not(wanted))
    def _():
        full_acc[...] = full_in[...]
        cross_acc[...] = jnp.zeros_like(cross_acc)
        value_acc[...] = value_in[...]
        if kind == 1:
            value_acc[pl.ds(own_rows, own_rows), :] = jnp.zeros((own_rows, LANES), F32)

    def some_ref(s):
        return some_in if s == 0 else cross_acc

    def full_grad(k, s, lanes):
        return full_acc[full_at(k, s), lanes]

    def some_grad(k, s, lanes):
        return some_ref(s)[some_at(k, s), lanes]

    (query_grad, key_grad) = (some_grad, full_grad) if kind == 0 else (full_grad, some_grad)
    query_count, key_count = ((2, members) if kind == 0 else (members, 2))
    low, high = (slice(0, LANES), slice(LANES, 2 * LANES))

    def value_grad(k, s):
        if kind == 0:
            return value_acc[full_at(k, s), :]
        return value_acc[pl.ds((s * heads + k) * rows, rows), :]

    lane = iota((rows, LANES), 1)
    half = 8 * heads
    for m, sums_ref in enumerate(sums_refs):
        sums = jnp.zeros((rows, LANES), F32)
        for k in range(heads):
            for s in range(8 * m, min(8 * m + 8, query_count)):
                at = (s - 8 * m) * heads + k
                sums = jnp.where(lane == at, query_grad(k, s, high), sums)
            for s in range(8 * m, min(8 * m + 8, key_count)):
                at = half + (s - 8 * m) * heads + k
                sums = jnp.where(lane == at, -key_grad(k, s, high), sums)
        sums_ref[...] = sums
    blank = jnp.zeros((rows, LANES), BF16)
    for k in range(heads):
        dq_own[k] = query_grad(k, 0, low)
        dk_own[k] = key_grad(k, 0, low)
        dv_own[k] = value_grad(k, 0)
        sends = [(to_cross, 1, kind == 1)]
        sends += [(to_peer[s - 1], s, kind == 0) for s in range(1, members)]
        for ref, s, keys in sends:
            ref[k, 0:rows, :] = (key_grad(k, s, low) if keys else query_grad(k, s, low)).astype(BF16)
            ref[k, rows : 2 * rows, :] = value_grad(k, s).astype(BF16) if keys else blank


def suffix_kernel(plan, *refs):
    rows, heads, members, scale = plan
    chunks = -(-members // 8)
    sums_refs, outs = (refs[:chunks], refs[chunks:])
    place = place_of(heads, members)
    bases = place[BASE:]
    first_kind = place[KIND] == 0
    count = 2 * members
    half = 8 * heads
    square = (LANES, LANES)
    shape = (count * heads, LANES)
    target_pos = block_positions(bases, shape, 0, heads, members, 0, range(count))
    onward = (iota(square, 0) >= iota(square, 1)).astype(F32)
    later, inner = (jnp.zeros(shape, F32), jnp.zeros(shape, F32))
    pair = [0, members]
    for m, sums_ref in enumerate(sums_refs):
        turned = pad_rows(sums_ref[...]).T
        some = pair if m == 0 else []
        full = range(8 * m, min(8 * m + 8, members))
        slot_pos = [
            jnp.maximum(
                block_positions(bases, (8, LANES), 1, heads, members, 0, queries),
                block_positions(bases, (8, LANES), 1, heads, members, half, keys),
            )[0:1]
            for queries, keys in ((some, full), (full, some))
        ]
        slot_pos = jnp.where(first_kind, slot_pos[0], slot_pos[1])
        later += dot_exact((slot_pos > target_pos).astype(F32), turned)
        inner += dot_exact((slot_pos == target_pos).astype(F32), turned)
    suffix = jnp.sum(later, axis=1, keepdims=True) + dot_exact(inner, onward)
    for src, ref in enumerate(outs):
        ref[...] = suffix[src * heads : (src + 1) * heads]


def combine_kernel(plan, keep_ref, dq_ref, dk_ref, dv_ref, cross, *refs):
    rows, heads, members, scale = plan
    peers, gate_refs, out_ref = (refs[: members - 1], refs[members - 1 : -1], refs[-1])
    first_kind = place_of(heads, members)[KIND] == 0
    gates = gate_refs[0][...]
    for ref in gate_refs[1:]:
        gates += ref[...]
    gates *= keep_ref[...]
    for k in range(heads):
        far = cross[k].astype(F32)
        near = peers[0][k].astype(F32)
        for ref in peers[1:]:
            near += ref[k].astype(F32)
        to_keys = jnp.where(first_kind, near, far)
        to_queries = jnp.where(first_kind, far[0:rows], near[0:rows])
        out_ref[k, 0:rows, :] = (scale * (dq_ref[k] + to_queries)).astype(BF16)
        out_ref[k, rows : 2 * rows, :] = (scale * (dk_ref[k] + to_keys[0:rows])).astype(BF16)
        out_ref[k, 2 * rows : 3 * rows, :] = (dv_ref[k] + to_keys[rows:]).astype(BF16)
        out_ref[k, 3 * rows :, :] = jnp.broadcast_to(gates[k : k + 1], (STAT, LANES)).astype(BF16)


def unpack_kernel(in_ref, dq_ref, dk_ref, dv_ref, gate_ref):
    rows = dq_ref.shape[0]
    heads = in_ref.shape[0]
    gates = []
    for h in range(heads):
        cols = pl.ds(h * LANES, LANES)
        dq_ref[:, cols] = in_ref[h, 0:rows, :]
        dk_ref[:, cols] = in_ref[h, rows : 2 * rows, :]
        dv_ref[:, cols] = in_ref[h, 2 * rows : 3 * rows, :]
        gates.append(in_ref[h, 3 * rows :, :].astype(F32)[0:1])
    gate_ref[...] = jnp.concatenate(gates, axis=0)[:, 0:rows].astype(BF16)


def struct(shape, dtype=BF16):
    return jax.ShapeDtypeStruct(shape, dtype)


def call(kernel, out_shape, inputs, scratch=(), space=VMEM, limit=40, flops=None):
    return pl.pallas_call(
        kernel,
        out_shape=out_shape,
        in_specs=[space] * len(inputs),
        out_specs=jax.tree.map(lambda _: VMEM, out_shape),
        scratch_shapes=list(scratch),
        cost_estimate=None if flops is None else pl.CostEstimate(flops=flops, bytes_accessed=0, transcendentals=0),
        compiler_params=pltpu.CompilerParams(vmem_limit_bytes=int(limit * 1024 * 1024)),
    )(*inputs)


def per_device(queries, key_inputs, value_inputs, out_grad, attn_output, gate_logits, lse):
    ctx, group = (lax.axis_size("ctx"), lax.axis_size("head"))
    rows, heads = gate_logits.shape
    width = queries.shape[1]
    scale = (width // heads) ** -0.5
    half = ctx * group // 2
    members = half // heads
    both = ("ctx", "head")

    def device(side, slot, member):
        return side * half + slot * members + member

    def shift(array, across, along, chosen):
        pairs = [
            (device(side ^ across, slot, (member + along) % members), device(side, slot, member))
            for side in (0, 1)
            for slot in range(heads)
            for member in range(members)
            if chosen(side, int(slot >= heads // 2))
        ]
        return lax.ppermute(array, both, pairs)

    def everyone(side, kind):
        return True

    def working(side, kind):
        return side == kind

    def waiting(side, kind):
        return side != kind

    regions = [
        [device(side, slot, member) for slot in range(heads)] for side in (0, 1) for member in range(members)
    ]

    def exchange(array):
        return lax.all_to_all(
            array, both, split_axis=0, concat_axis=0, axis_index_groups=regions, tiled=True
        )

    kind = place_of(heads, members)[KIND]

    packed = call(
        pack_kernel,
        struct((heads, 4 * rows + STAT, LANES)),
        (queries, key_inputs, value_inputs, out_grad, attn_output, gate_logits.T, lse.T),
        scratch=[pltpu.VMEM((rows, width), BF16)] * 5
        + [pltpu.VMEM((heads, rows), BF16), pltpu.VMEM((heads, rows), F32)]
        + [pltpu.VMEM((heads, LANES), F32)] * 2
        + [pltpu.SemaphoreType.DMA((7,))],
        space=HBM,
        limit=PACK_LIMIT,
    )
    own = exchange(packed)
    length = 2 * rows + STAT

    cross_send = lax.dynamic_slice_in_dim(own, jnp.where(kind == 1, 2 * rows, 0), length, axis=1)
    peer_send = lax.dynamic_slice_in_dim(own, jnp.where(kind == 0, length, 0), 2 * rows, axis=1)
    stat_send = own[:, 2 * rows : length]
    gate_send = own[:, 2 * rows]
    cross = shift(cross_send, 1, 0, working)
    peers = [shift(peer_send, 0, s, everyone) for s in range(1, members)]
    peer_stats = [shift(stat_send, 0, s, everyone) for s in range(1, members)]
    corner = [shift(gate_send, 1, s, working) for s in range(1, members)]

    plan = (rows, heads, members, scale)
    own_rows, full_rows = (heads * rows, heads * members * rows)
    value_rows = max(full_rows, 2 * own_rows)
    wide = 2 * LANES
    small = struct((heads, LANES), F32)
    *state, keep = call(
        functools.partial(own_kernel, plan),
        [
            struct((full_rows, wide)),
            struct((full_rows, wide)),
            struct((full_rows, wide), F32),
            struct((own_rows, wide), F32),
            struct((value_rows, LANES), F32),
            small,
            small,
        ],
        (own, *peers, *peer_stats),
        scratch=[pltpu.VMEM((own_rows, wide), BF16)] * 2,
    )
    piece = struct((heads, rows, LANES), F32)
    sent = struct((heads, 2 * rows, LANES))
    chunks = -(-members // 8)
    dq, dk, dv, to_cross, *others = call(
        functools.partial(square_kernel, plan),
        [piece, piece, piece, sent] + [sent] * (members - 1) + [struct((rows, LANES), F32)] * chunks,
        (*state, cross, *corner),
        scratch=[pltpu.VMEM((own_rows, wide), BF16)] * 2
        + [
            pltpu.VMEM((full_rows, wide), F32),
            pltpu.VMEM((own_rows, wide), F32),
            pltpu.VMEM((value_rows, LANES), F32),
        ],
    )
    to_peer, sums = (others[: members - 1], others[members - 1 :])
    cross = shift(to_cross, 1, 0, waiting)
    peers = [shift(to_peer[s - 1], 0, members - s, everyone) for s in range(1, members)]
    gates = call(functools.partial(suffix_kernel, plan), [small] * (2 * members), tuple(sums))
    gates = (
        [gates[0]]
        + [shift(gates[s], 0, members - s, everyone) for s in range(1, members)]
        + [shift(gates[members + s], 1, (members - s) % members, waiting) for s in range(members)]
    )
    summed = call(
        functools.partial(combine_kernel, plan),
        struct((heads, 3 * rows + STAT, LANES)),
        (keep, dq, dk, dv, cross, *peers, *gates),
    )
    final = exchange(summed)
    full = struct(queries.shape)
    dq, dk, dv, gate_grad = call(unpack_kernel, [full, full, full, struct((heads, rows))], (final,))
    return dq, dk, dv, gate_grad.T


def solution(mesh):
    split = P(("ctx", "head"), None)
    return jax.shard_map(
        per_device,
        mesh=mesh,
        in_specs=(split,) * 7,
        out_specs=(split,) * 4,
        check_vma=False,
    )
```
